128 devices in a mesh: ctx: 16 (over z, x), enc: 8 (over y, core).
Axes of the slice: x: 4, y: 4, z: 4, core: 2. Of those that a mesh axis runs over, the one named last changes fastest.
Arguments:
- queries: bfloat16 [4096, 8192], P('ctx', 'enc'), may hold values from -6 to 6
- out_grad: bfloat16 [4096, 8192], P('ctx', 'enc'), may hold values from -6 to 6
- nbr_states: bfloat16 [64, 128, 2048], P('ctx', None, 'enc'), may hold values from -6 to 6
- key_weight: bfloat16 [2048, 8192], P('ctx', 'enc'), may hold values from -0.125 to 0.125
- value_weight: bfloat16 [2048, 8192], P('ctx', 'enc'), may hold values from -0.125 to 0.125
- q_gain: float32 [8192], P('enc'), may hold values from 0.25 to 1.75
- k_gain: float32 [8192], P('enc'), may hold values from 0.25 to 1.75
- nbr_owner: int32 [64, 2], replicated, may hold values from 0 to 15, all different within a row; in each aligned block of 4 rows (0 to 3, 4 to 7, ...) at most 2 rows name the same one
- nbr_slot: int32 [64, 2], replicated, may hold values from 0 to 3
Outputs:
- query_grad: bfloat16 [4096, 8192], P('ctx', 'enc')
- state_grad: float32 [64, 128, 2048], P('ctx', None, 'enc')
The draws below stay inside these ranges and needn't reach their ends.
Inputs may be any that keep to these rules, and one draw needn't show every extreme that they name: `nbr_owner`: within the 4 spans of one ctx index (aligned blocks of spans), no owner is named more than 2 times, a bound that some block reaches; a span's two neighbours have different owners.
All inputs are finite; a program needn't handle non-finite values.
Results may differ from the reference program's by a relative error of at most 0.018.
Values may be sent and summed in bfloat16 or wider, within the bound.
A program may use at most 192 MiB of HBM per device.

```python
import math
import jax
import jax.numpy as jnp
import numpy as np
from jax import lax

H = 64
DH = 128
DE = 2048
SPAN = 64
NT = 128
CAP = 2
CD = 4
POOL_DEV = 4
S = 4096
SPANS = 64
NPOOL = 64
HD = 8192
N_CTX = 16


def place_ends(result, rng, low, largest):
    place = [jax.random.randint(jax.random.fold_in(rng, axis), (), 0, length) for axis, length in enumerate(result.shape)]
    longest = result.shape.index(max(result.shape))
    neighbour = place[:longest] + [(place[longest] + 1) % result.shape[longest]] + place[longest + 1:]
    return result.at[tuple(place)].set(low).at[tuple(neighbour)].set(largest)


def block_scale(key, extent, split, low, top_value):
    loudness = 1.0
    for axis_at, shards_of in split:
        heights = jax.random.uniform(jax.random.fold_in(jax.random.fold_in(key, 6), axis_at), (shards_of,), jnp.float32, low / len(split), top_value / len(split))
        loudness = loudness * jnp.repeat(jnp.exp(heights), extent[axis_at] // shards_of).reshape((-1,) + (1,) * (len(extent) - 1 - axis_at))
    return loudness


def deal_out(rng, own, number, rows, number_of, top, limit, slope):
    sequence = jax.random.permutation(rng, number_of)
    crowded, ordinary = load_shares(number_of, rows * top, limit, slope, True), load_shares(number_of, rows * top, limit, slope, False)
    places = jnp.arange(number_of)

    def named(lengths, turn):
        used = int((lengths > 0).sum())
        fixed = max(1, used // 4)
        passed = fixed + (places - fixed + turn * (used - fixed)) % max(1, number_of - fixed)
        return jnp.zeros((number_of,), jnp.int32).at[sequence[jnp.where(places < fixed, places, passed)]].set(jnp.asarray(lengths, jnp.int32))

    lengths = jnp.where(number % 4 == 0, named(crowded, number // 4), named(ordinary, number - number // 4 - 1))
    mixed = jax.random.permutation(jax.random.fold_in(own, 3), number_of)
    giver, receiver = mixed[0:number_of // 2 * 2:2], mixed[1:number_of // 2 * 2:2]
    room = jnp.minimum(lengths[giver] - 1, limit - lengths[receiver]) // 2
    room = jnp.where((giver == sequence[0]) | (receiver == sequence[0]) | (lengths[receiver] == 0), 0, jnp.maximum(room, 0))
    passed = jax.random.randint(jax.random.fold_in(own, 4), (number_of // 2,), 0, 1 << 20) % (room + 1)
    lengths = lengths.at[giver].add(-passed).at[receiver].add(passed)
    items = jnp.searchsorted(jnp.cumsum(lengths), jnp.arange(rows * top), side="right").astype(jnp.int32)
    table = items.reshape(top, rows).T
    table = table[jax.random.permutation(jax.random.fold_in(own, 1), rows)]
    turn = jax.random.randint(jax.random.fold_in(own, 2), (rows, 1), 0, top)
    return jnp.take_along_axis(table, (jnp.arange(top)[None, :] + turn) % top, axis=1)


def load_shares(number_of, total, limit, lean, full):
    portions = [(1 << 20) // math.isqrt(grade ** lean) + 1 for grade in range(1, number_of + 1)]
    largest = limit if full else min(limit, max(-(-total // number_of), total * portions[0] // sum(portions)))
    least = 1 if total - largest >= number_of - 1 else 0
    holding, rest = [largest] + [least] * (number_of - 1), total - largest - least * (number_of - 1)
    while rest > 0:
        free = [i for i in range(1, number_of) if holding[i] < largest] or [i for i in range(1, number_of) if holding[i] < limit]
        mass, left = sum([portions[i] for i in free]), rest
        for i in free:
            more = min(limit - holding[i], max(1, left * portions[i] // mass), rest)
            holding[i] = holding[i] + more
            rest = rest - more
    return np.array(holding)


def scatter_about(stream_key, shape, deviation, bound, cuts=(), kind=jnp.bfloat16):
    factor_of = block_scale(stream_key, shape, cuts, -0.22, 0.18) if cuts else 1.0
    values = jax.random.normal(stream_key, shape, jnp.float32) * deviation * factor_of
    return jnp.minimum(jnp.maximum(values, -bound), bound).astype(kind)


def setup_inputs(seed: int = 0) -> dict:
    keys = jax.random.split(jax.random.key(seed), 10)
    queries = scatter_about(keys[0], (S, HD), 1.0, 6.0, ((0, 16), (1, 8)))
    out_grad = scatter_about(keys[1], (S, HD), 1.0, 6.0, ((0, 16), (1, 8)))
    nbr_states = scatter_about(keys[2], (NPOOL, NT, DE), 1.0, 6.0, ((0, 16), (2, 8)))
    key_weight = scatter_about(keys[3], (DE, HD), DE ** -0.5, 0.125, ((0, 16), (1, 8)))
    value_weight = scatter_about(keys[4], (DE, HD), DE ** -0.5, 0.125, ((0, 16), (1, 8)))
    q_gain = jnp.clip(1.0 + 0.15 * jax.random.normal(keys[5], (HD,), jnp.float32), 0.25, 1.75)
    k_gain = jnp.clip(1.0 + 0.15 * jax.random.normal(keys[6], (HD,), jnp.float32), 0.25, 1.75)
    nbr_owner_keys = jax.random.split(jax.random.fold_in(keys[7], 1), SPANS // CD)
    nbr_owner_turns = jax.random.permutation(jax.random.fold_in(keys[7], 3), SPANS // CD)
    nbr_owner = jax.vmap(lambda own, number: deal_out(jax.random.fold_in(keys[7], 2), own, number, CD, N_CTX, 2, CAP, 2))(nbr_owner_keys, nbr_owner_turns).reshape((SPANS, 2))
    nbr_slot = place_ends(jax.random.randint(keys[8], (SPANS, 2), 0, POOL_DEV), jax.random.fold_in(keys[8], 1), 0, POOL_DEV - 1).astype(jnp.int32)
    return {"queries": queries, "out_grad": out_grad, "nbr_states": nbr_states, "key_weight": key_weight, "value_weight": value_weight, "q_gain": q_gain, "k_gain": k_gain, "nbr_owner": nbr_owner, "nbr_slot": nbr_slot}


PRECISE = lax.Precision.HIGHEST
EPSILON = 1e-06
LOG_BASE = 9.210340371976184

def normalize(tensor):
    return tensor * lax.rsqrt(lax.optimization_barrier(jnp.mean(tensor * tensor, axis=-1, keepdims=True)) + EPSILON)

def rotate(tensor, positions):
    halved = tensor.shape[-1] // 2
    exponents = jnp.arange(halved).astype(jnp.float32)
    frequency = jnp.exp(exponents * (-2.0 * LOG_BASE / tensor.shape[-1]))
    angles = positions.astype(jnp.float32)[:, None] * frequency[None, :]
    cosine = jnp.cos(angles)[:, None, :]
    sine_part = jnp.sin(angles)[:, None, :]
    first_half = tensor[..., :halved]
    second_half = tensor[..., halved:]
    return jnp.concatenate([first_half * cosine - second_half * sine_part, first_half * sine_part + second_half * cosine], axis=-1)

def attend(query_win, key_win, value_win, query_scale, key_scale):
    query_rot = rotate(normalize(query_win) * query_scale, jnp.arange(query_win.shape[1]))
    key_rot = rotate(normalize(key_win) * key_scale, jnp.arange(key_win.shape[1]) % NT)
    scores = jnp.einsum('wqhd,wkhd->whqk', query_rot, key_rot, precision=PRECISE) * query_win.shape[-1] ** (-0.5)
    weights = jax.nn.softmax(scores, axis=-1)
    return jnp.einsum('whqk,wkhd->wqhd', weights, value_win, precision=PRECISE)

def reference(queries, out_grad, nbr_states, key_weight, value_weight, q_gain, k_gain, nbr_owner, nbr_slot):
    pool_index = (nbr_owner * POOL_DEV + nbr_slot).reshape(-1).astype(jnp.int32)
    fetched = jnp.take(nbr_states, pool_index, axis=0).reshape(SPANS * 2 * NT, DE)
    key_pre = jnp.dot(fetched, key_weight, preferred_element_type=jnp.float32).astype(jnp.bfloat16)
    value_pre = jnp.dot(fetched, value_weight, preferred_element_type=jnp.float32).astype(jnp.bfloat16)
    key_win = key_pre.astype(jnp.float32).reshape(SPANS, 2 * NT, H, DH)
    value_win = value_pre.astype(jnp.float32).reshape(SPANS, 2 * NT, H, DH)
    padding = jnp.zeros((SPAN - 1, H * DH), jnp.bfloat16)
    query_win = jnp.concatenate([queries[SPAN - 1:], padding]).astype(jnp.float32).reshape(SPANS, SPAN, H, DH)
    grad_win = jnp.concatenate([out_grad[SPAN - 1:], padding]).astype(jnp.float32).reshape(SPANS, SPAN, H, DH)
    query_scale = q_gain.reshape(H, DH)
    key_scale = k_gain.reshape(H, DH)

    def attend_here(query_arg, key_arg, value_arg):
        return attend(query_arg, key_arg, value_arg, query_scale, key_scale)
    attended, pullback = jax.vjp(attend_here, query_win, key_win, value_win)
    grad_query, grad_key, grad_value = pullback(grad_win)
    leading = jnp.zeros((SPAN - 1, H * DH), jnp.float32)
    query_grad = jnp.concatenate([leading, grad_query.reshape(S, H * DH)[:S - SPAN + 1]]).astype(jnp.bfloat16)
    key_grad = grad_key.reshape(SPANS * 2 * NT, H * DH).astype(jnp.bfloat16)
    value_grad = grad_value.reshape(SPANS * 2 * NT, H * DH).astype(jnp.bfloat16)
    ref_grad = jnp.dot(key_grad, key_weight.T, preferred_element_type=jnp.float32) + jnp.dot(value_grad, value_weight.T, preferred_element_type=jnp.float32)
    state_grad = jnp.zeros((NPOOL, NT, DE), jnp.float32).at[pool_index].add(ref_grad.reshape(SPANS * 2, NT, DE))
    return (query_grad, state_grad)
```

```python
import functools

import jax
import jax.numpy as jnp
import numpy as np
from jax import lax
from jax.experimental import pallas as pl
from jax.experimental.pallas import tpu as pltpu
from jax.sharding import PartitionSpec as P

MESH = pl.DeviceIdType.MESH
F32 = jnp.float32
BF16 = jnp.bfloat16

DH = 128
SPAN = 64
NT = 128
EPSILON = 1e-06
LOG_BASE = 9.210340371976184
SCALE = DH**-0.5
CHUNKS = 4
CW = 256

NT_DIMS = (((1,), (1,)), ((), ()))
TN_DIMS = (((0,), (0,)), ((), ()))


def rope_tables():
    half = DH // 2
    freq = np.exp(np.arange(half) * (-2.0 * LOG_BASE / DH))
    angle = np.arange(NT)[:, None] * freq[None, :]
    cos = np.concatenate([np.cos(angle)] * 2, axis=1)
    sin = np.concatenate([-np.sin(angle), np.sin(angle)], axis=1)
    twice = lambda t: np.concatenate([t, t], axis=0).astype(np.float32)
    return twice(cos), twice(sin)


def swap(v):
    return pltpu.roll(v, DH // 2, 1)


def unit(v):
    r = lax.rsqrt(jnp.mean(v * v, axis=1, keepdims=True) + EPSILON)
    return v * r, r


def rope(v, cos, sin):
    return v * cos + swap(v) * sin


def rope_back(d, cos, sin):
    return d * cos + swap(d * sin)


def unit_back(d, xhat, r):
    return r * (d - xhat * jnp.mean(d * xhat, axis=1, keepdims=True))


def kernel(
    q_ref, do_ref, pool_ref, kw_ref, vw_ref, qg_ref, kg_ref, cos_ref, sin_ref, owner_ref, slot_ref,
    qgrad_ref, sgrad_ref,
    pool_all, kw_all, vw_all, ebuf, halo_out, halo, qwin, qbd, dobd, dqwin, qback_out, qback, dkv,
    sib_out, sib_in, own, t_out, t_in, m_out, m_in, refg, ret_out, ret_in, stab,
    ag_s, ag_r, e_s, e_r, sib_s, sib_r, h_s, h_r, rs_s, rs_r, a2a_s, a2a_r,
):
    c, e = lax.axis_index("ctx"), lax.axis_index("enc")
    z, x = c // 4, c % 4
    y, core = e // 2, e % 2
    up, dn = (y + 1) % 4, (y + 3) % 4
    enc = lambda y_, core_: y_ * 2 + core_
    pending = []

    def send(src, dst, ssem, rsem, dev):
        cp = pltpu.make_async_remote_copy(
            src_ref=src, dst_ref=dst, send_sem=ssem, recv_sem=rsem, device_id=dev, device_id_type=MESH
        )
        cp.start()
        pending.append(cp)
        return cp

    barrier = pltpu.get_barrier_semaphore()
    for d in range(1, 16):
        pl.semaphore_signal(barrier, inc=1, device_id=((c + d) % 16, e), device_id_type=MESH)
    for other in (enc(up, core), enc(dn, core), enc(y, 1 - core)):
        pl.semaphore_signal(barrier, inc=1, device_id=(c, other), device_id_type=MESH)
    pl.semaphore_wait(barrier, 18)

    class Item:
        def __init__(self, n, bufs, blocks):
            self.n, self.bufs, self.blocks = n, bufs, blocks
            self.cp = {}

        def view(self, ab, first, second):
            zi, xi = (second, first) if ab == 0 else (first, second)
            ref = self.bufs[ab]
            if self.blocks[ab] is None:
                return ref.at[zi, xi]
            return ref.at[zi, xi, self.blocks[ab]]

        def half(self, ab, first, second, h):
            zi, xi = (second, first) if ab == 0 else (first, second)
            ref = self.bufs[ab]
            if self.blocks[ab] is None:
                return ref.at[zi, xi, pl.ds(64 * h, 64)]
            return ref.at[zi, xi, pl.ds(self.blocks[ab].start + h, 1)]

        def coords(self, ab):
            return (x, z) if ab == 0 else (z, x)

        def dev(self, ab, first, second):
            return (second * 4 + first, e) if ab == 0 else (first * 4 + second, e)

        def go(self, step, ab, d, ref, to):
            self.cp[step, ab, d] = send(
                ref, ref, ag_s.at[self.n, ab, step, d], ag_r.at[self.n, ab, step, d], to
            )

        def s1(self):
            for ab in (0, 1):
                f, s = self.coords(ab)
                for d in (0, 1):
                    to = self.dev(ab, (f + (1, 3)[d]) % 4, s)
                    self.go(0, ab, d, self.view(ab, f, s), to)

        def s2(self):
            for ab in (0, 1):
                f, s = self.coords(ab)
                for d in (0, 1):
                    self.cp[0, ab, d].wait_recv()
                    to = self.dev(ab, (f + (1, 3)[d]) % 4, s)
                    self.go(1, ab, d, self.half(ab, (f + (3, 1)[d]) % 4, s, d), to)

        def s3(self):
            for ab in (0, 1):
                f, s = self.coords(ab)
                for d in (0, 1):
                    self.cp[1, ab, d].wait_recv()
                for d in (0, 1):
                    to = self.dev(ab, f, (s + (1, 3)[d]) % 4)
                    self.go(2, ab, d, self.view(ab, pl.ds(0, 4), s), to)

        def s4(self):
            for ab in (0, 1):
                f, s = self.coords(ab)
                for d in (0, 1):
                    self.cp[2, ab, d].wait_recv()
                    to = self.dev(ab, f, (s + (1, 3)[d]) % 4)
                    self.go(3, ab, d, self.view(ab, pl.ds(2 * d, 2), (s + (3, 1)[d]) % 4), to)

        def done(self):
            for ab in (0, 1):
                for d in (0, 1):
                    self.cp[3, ab, d].wait_recv()

    pool = Item(0, (pool_all, pool_all), (pl.ds(0, 2), pl.ds(2, 2)))
    w = [Item(1 + j, (kw_all.at[j], vw_all.at[j]), (None, None)) for j in range(CHUNKS)]

    pool_all[z, x] = pool_ref[...]
    pool.s1()
    halo_out[0] = q_ref[0:SPAN, :]
    halo_out[1] = do_ref[0:SPAN, :]
    halo_cp = send(halo_out, halo, h_s.at[0], h_r.at[0], ((c + 15) % 16, e))
    for j in range(CHUNKS):
        kw_all[j, z, x] = kw_ref[:, j * CW : (j + 1) * CW]
        vw_all[j, z, x] = vw_ref[:, j * CW : (j + 1) * CW]
    w[0].s1()
    pool.s2()
    pool.s3()

    def table(p, _):
        first, last, count = jnp.int32(0), jnp.int32(0), jnp.int32(0)
        r_first, r_last, r_count = jnp.int32(0), jnp.int32(0), jnp.int32(0)
        for r in range(8):
            hit = owner_ref[c * 4 + r // 2, r % 2] == p
            first = jnp.where(hit & (count == 0), r, first)
            last = jnp.where(hit, r, last)
            count = count + hit.astype(jnp.int32)
            there = owner_ref[p * 4 + r // 2, r % 2] == c
            n = slot_ref[p * 4 + r // 2, r % 2]
            r_first = jnp.where(there & (r_count == 0), n, r_first)
            r_last = jnp.where(there, n, r_last)
            r_count = r_count + there.astype(jnp.int32)
        stab[0, p], stab[1, p], stab[2, p] = first, last, count
        stab[3, p] = jnp.where(r_count > 0, r_first, -1)
        stab[4, p] = jnp.where(r_count > 1, r_last, -1)
        return 0

    lax.fori_loop(0, 16, table, 0)

    halo_cp.wait_recv()
    keep = jnp.where(c == 15, 0.0, 1.0)
    first_row = lax.broadcasted_iota(jnp.int32, (4 * SPAN, DH), 0) == 0

    def windows(ref, which, cols):
        own_rows = ref[:, cols].astype(F32)
        nxt = halo[which, :, cols].astype(F32) * keep
        shifted = pltpu.roll(jnp.concatenate([own_rows[SPAN:], nxt], axis=0), 1, 0)
        return jnp.where(first_row, own_rows[SPAN - 1 : SPAN], shifted)

    qcos = jnp.concatenate([cos_ref[0:SPAN, :]] * 4, axis=0)
    qsin = jnp.concatenate([sin_ref[0:SPAN, :]] * 4, axis=0)
    zero = jnp.zeros((SPAN, DH), BF16)

    def prepare(h):
        j, hh = h // 2, h % 2
        cols = pl.ds(h * DH, DH)
        v = windows(q_ref, 0, cols)
        qwin[h] = v
        xhat, _ = unit(v)
        rot = (rope(xhat * qg_ref[:, cols], qcos, qsin) * SCALE).astype(BF16)
        dov = windows(do_ref, 1, cols).astype(BF16)
        for s in range(4):
            r = slice(s * SPAN, (s + 1) * SPAN)
            mine = slice(hh * DH, (hh + 1) * DH)
            rest = slice((1 - hh) * DH, (2 - hh) * DH)
            rows = slice(hh * SPAN, (hh + 1) * SPAN)
            qbd[j, s, rows, mine] = rot[r]
            qbd[j, s, rows, rest] = zero
            dobd[j, s, rows, mine] = dov[r]
            dobd[j, s, rows, rest] = zero

    for h in range(8):
        prepare(h)

    w[0].s2()
    w[1].s1()
    pool.s4()
    w[0].s3()
    pool.done()

    for r in range(8):
        o, n = owner_ref[c * 4 + r // 2, r % 2], slot_ref[c * 4 + r // 2, r % 2]
        ebuf[e, r * NT : (r + 1) * NT, :] = pool_all[o // 4, o % 4, n]

    ring = {}
    sib = {}
    for d, to in ((0, up), (1, dn)):
        ring[0, d] = send(ebuf.at[e], ebuf.at[e], e_s.at[0, d], e_r.at[0, d], (c, enc(to, core)))
    other = (c, enc(y, 1 - core))

    def to_sibling(i, slot):
        sib[i] = send(ebuf.at[slot], ebuf.at[slot], sib_s.at[i], sib_r.at[i], other)

    to_sibling(0, e)
    w[1].s2()
    w[2].s1()
    w[0].s4()
    w[1].s3()
    for d, frm, to in ((0, dn, up), (1, up, dn)):
        ring[0, d].wait_recv()
        slot = enc(frm, core)
        part = ebuf.at[slot, pl.ds(512 * d, 512)]
        ring[1, d] = send(part, part, e_s.at[1, d], e_r.at[1, d], (c, enc(to, core)))
        to_sibling(1 + d, slot)
    w[2].s2()
    w[3].s1()
    for d in (0, 1):
        ring[1, d].wait_recv()
    to_sibling(3, enc((y + 2) % 4, core))
    w[1].s4()
    w[2].s3()
    w[3].s2()
    for i in range(4):
        sib[i].wait_recv()

    def compute(j):
        kw = kw_all[j].reshape(2048, CW)
        vw = vw_all[j].reshape(2048, CW)

        def span(s, _):
            rows = pl.ds(pl.multiple_of(s * 256, 256), 256)
            ecat = jnp.concatenate([ebuf[i, rows, :] for i in range(8)], axis=1)
            kp = jnp.dot(ecat, kw, preferred_element_type=F32).astype(BF16).astype(F32)
            vp = jnp.dot(ecat, vw, preferred_element_type=F32).astype(BF16)
            cos, sin = cos_ref[...], sin_ref[...]
            hats, rs, gains, ks = [], [], [], []
            for hh in range(2):
                xhat, r = unit(kp[:, hh * DH : (hh + 1) * DH])
                g = kg_ref[:, (2 * j + hh) * DH : (2 * j + hh + 1) * DH]
                ks.append(rope(xhat * g, cos, sin).astype(BF16))
                hats.append(xhat)
                rs.append(r)
                gains.append(g)
            k = jnp.concatenate(ks, axis=1)
            qb, dob = qbd[j, s], dobd[j, s]
            scores = lax.dot_general(k, qb, NT_DIMS, preferred_element_type=F32)
            dp = lax.dot_general(vp, dob, NT_DIMS, preferred_element_type=F32)
            p = jnp.exp(scores)
            p = p * (1.0 / jnp.sum(p, axis=0, keepdims=True))
            ds = (p * (dp - jnp.sum(p * dp, axis=0, keepdims=True))).astype(BF16)
            dv = jnp.dot(p.astype(BF16), dob, preferred_element_type=F32)
            dk = jnp.dot(ds, qb, preferred_element_type=F32)
            dq = lax.dot_general(ds, k, TN_DIMS, preferred_element_type=F32) * SCALE
            base = j * 512
            for hh in range(2):
                cols = slice(hh * DH, (hh + 1) * DH)
                d = rope_back(dk[:, cols], cos, sin) * gains[hh]
                dkv[rows, base + hh * DH : base + (hh + 1) * DH] = unit_back(d, hats[hh], rs[hh]).astype(BF16)
            dkv[rows, base + 256 : base + 512] = dv.astype(BF16)
            qrows = pl.ds(pl.multiple_of(s * SPAN, SPAN), SPAN)
            for hh in range(2):
                h = 2 * j + hh
                xhat, r = unit(qwin[h, qrows, :])
                d = dq[hh * SPAN : (hh + 1) * SPAN, hh * DH : (hh + 1) * DH]
                d = rope_back(d, cos_ref[0:SPAN, :], sin_ref[0:SPAN, :]) * qg_ref[:, h * DH : (h + 1) * DH]
                dqwin[qrows, h * DH : (h + 1) * DH] = unit_back(d, xhat, r)
            return 0

        lax.fori_loop(0, 4, span, 0)

    w[0].done()
    compute(0)
    w[2].s4()
    w[3].s3()
    w[1].done()
    compute(1)
    w[3].s4()
    w[2].done()
    compute(2)
    w[3].done()
    compute(3)

    def shifted_back(cols):
        return pltpu.roll(dqwin[:, cols], 4 * SPAN - 1, 0)

    for h in range(8):
        cols = slice(h * DH, (h + 1) * DH)
        back = shifted_back(cols).astype(BF16)
        qgrad_ref[SPAN:, cols] = back[: 3 * SPAN]
        qback_out[:, cols] = back[3 * SPAN :]
    qback_cp = send(qback_out, qback, h_s.at[1], h_r.at[1], ((c + 1) % 16, e))

    rs_cp = {}

    def product(f, which, out):
        xi = 2 * which + f
        wcat = jnp.concatenate(
            [b[j, :, xi].reshape(512, CW) for j in range(CHUNKS) for b in (kw_all, vw_all)], axis=1
        )

        def span(s, _):
            rows = pl.ds(pl.multiple_of(s * 256, 256), 256)
            part = lax.dot_general(dkv[rows, :], wcat, NT_DIMS, preferred_element_type=F32)
            for i in range(4):
                out[f, i, rows, :] = part[:, i * 128 : (i + 1) * 128].astype(out.dtype)
            return 0

        lax.fori_loop(0, 4, span, 0)

    def rs_a(f):
        product(f, 1 - core, sib_out)
        rs_cp[f, 0] = send(sib_out.at[f], sib_in.at[f], rs_s.at[f, 0], rs_r.at[f, 0], other)
        product(f, core, own)

    def rs_b(f):
        rs_cp[f, 0].wait_recv()
        opp = (y + 2) % 4
        for d, to in ((0, up), (1, dn)):
            rows = slice(512 * d, 512 * d + 512)
            t_out[f, d] = (own[f, opp, rows, :] + sib_in[f, opp, rows, :].astype(F32)).astype(BF16)
            rs_cp[f, 1, d] = send(
                t_out.at[f, d], t_in.at[f, d], rs_s.at[f, 1 + d], rs_r.at[f, 1 + d], (c, enc(to, core))
            )

    def rs_c(f):
        for d, to in ((0, up), (1, dn)):
            rs_cp[f, 1, d].wait_recv()
            rows = slice(512 * d, 512 * d + 512)
            rest = slice(512 - 512 * d, 1024 - 512 * d)
            both = lambda r: own[f, to, r, :] + sib_in[f, to, r, :].astype(F32)
            m_out[f, d, rows, :] = (both(rows) + t_in[f, d].astype(F32)).astype(BF16)
            m_out[f, d, rest, :] = both(rest).astype(BF16)
            rs_cp[f, 2, d] = send(
                m_out.at[f, d], m_in.at[f, d], rs_s.at[f, 3 + d], rs_r.at[f, 3 + d], (c, enc(to, core))
            )

    def rs_d(f):
        for d in (0, 1):
            rs_cp[f, 2, d].wait_recv()
        for r in range(8):
            rows = slice(r * NT, (r + 1) * NT)
            refg[f, r] = (
                own[f, y, rows, :]
                + sib_in[f, y, rows, :].astype(F32)
                + m_in[f, 0, rows, :].astype(F32)
                + m_in[f, 1, rows, :].astype(F32)
            )
        for d in range(16):
            p = (c + d) % 16
            count = stab[2, p]
            one = jnp.where(count > 0, 1.0, 0.0)
            two = jnp.where(count > 1, 1.0, 0.0)
            block0 = (refg[f, stab[0, p]] * one).astype(BF16)
            block1 = (refg[f, stab[1, p]] * two).astype(BF16)
            if d == 0:
                ret_in[f, c, 0] = block0
                ret_in[f, c, 1] = block1
                continue
            ret_out[f, d, 0] = block0
            ret_out[f, d, 1] = block1
            rs_cp[f, 3, d] = send(
                ret_out.at[f, d], ret_in.at[f, c], a2a_s.at[f, d], a2a_r.at[f, d], (p, e)
            )

    def rs_e(f):
        for d in range(1, 16):
            rs_cp[f, 3, d].wait_recv()

        def add(p, accs):
            b0, b1 = ret_in[f, p, 0].astype(F32), ret_in[f, p, 1].astype(F32)
            n0, n1 = stab[3, p], stab[4, p]
            return tuple(
                a + b0 * jnp.where(n0 == n, 1.0, 0.0) + b1 * jnp.where(n1 == n, 1.0, 0.0)
                for n, a in enumerate(accs)
            )

        for n, a in enumerate(lax.fori_loop(0, 16, add, tuple(jnp.zeros((NT, 128), F32) for _ in range(4)))):
            sgrad_ref[n, :, f * 128 : (f + 1) * 128] = a

    rs_a(0)
    rs_b(0)
    rs_a(1)
    rs_c(0)
    rs_b(1)
    rs_d(0)
    rs_c(1)
    rs_e(0)
    rs_d(1)

    qback_cp.wait_recv()
    live = jnp.where(c == 0, 0.0, 1.0)
    last_row = lax.broadcasted_iota(jnp.int32, (SPAN, DH), 0) == SPAN - 1
    for h in range(8):
        cols = slice(h * DH, (h + 1) * DH)
        head = qback[:, cols].astype(F32) * live
        qgrad_ref[0:SPAN, cols] = jnp.where(last_row, dqwin[0:1, cols], head).astype(BF16)

    rs_e(1)
    for cp in pending:
        cp.wait_send()


def shards(queries, out_grad, nbr_states, key_weight, value_weight, q_gain, k_gain, nbr_owner, nbr_slot):
    cos, sin = rope_tables()
    vmem = pl.BlockSpec(memory_space=pltpu.VMEM)
    smem = pl.BlockSpec(memory_space=pltpu.SMEM)
    dma = pltpu.SemaphoreType.DMA
    return pl.pallas_call(
        kernel,
        out_shape=(
            jax.ShapeDtypeStruct((256, 1024), BF16),
            jax.ShapeDtypeStruct((4, NT, 256), F32),
        ),
        in_specs=[vmem] * 9 + [smem] * 2,
        out_specs=(vmem, vmem),
        scratch_shapes=[
            pltpu.VMEM((4, 4, 4, NT, 256), BF16),
            pltpu.VMEM((CHUNKS, 4, 4, 128, CW), BF16),
            pltpu.VMEM((CHUNKS, 4, 4, 128, CW), BF16),
            pltpu.VMEM((8, 1024, 256), BF16),
            pltpu.VMEM((2, SPAN, 1024), BF16),
            pltpu.VMEM((2, SPAN, 1024), BF16),
            pltpu.VMEM((8, 4 * SPAN, DH), F32),
            pltpu.VMEM((4, 4, 2 * SPAN, 256), BF16),
            pltpu.VMEM((4, 4, 2 * SPAN, 256), BF16),
            pltpu.VMEM((4 * SPAN, 1024), F32),
            pltpu.VMEM((SPAN, 1024), BF16),
            pltpu.VMEM((SPAN, 1024), BF16),
            pltpu.VMEM((1024, 2048), BF16),
            pltpu.VMEM((2, 4, 1024, 128), BF16),
            pltpu.VMEM((2, 4, 1024, 128), BF16),
            pltpu.VMEM((2, 4, 1024, 128), F32),
            pltpu.VMEM((2, 2, 512, 128), BF16),
            pltpu.VMEM((2, 2, 512, 128), BF16),
            pltpu.VMEM((2, 2, 1024, 128), BF16),
            pltpu.VMEM((2, 2, 1024, 128), BF16),
            pltpu.VMEM((2, 8, NT, 128), F32),
            pltpu.VMEM((2, 16, 2, NT, 128), BF16),
            pltpu.VMEM((2, 16, 2, NT, 128), BF16),
            pltpu.SMEM((5, 16), jnp.int32),
            dma((1 + CHUNKS, 2, 4, 2)),
            dma((1 + CHUNKS, 2, 4, 2)),
            dma((2, 2)),
            dma((2, 2)),
            dma((4,)),
            dma((4,)),
            dma((2,)),
            dma((2,)),
            dma((2, 5)),
            dma((2, 5)),
            dma((2, 16)),
            dma((2, 16)),
        ],
        compiler_params=pltpu.CompilerParams(
            collective_id=0, has_side_effects=True, vmem_limit_bytes=60 * 2**20
        ),
    )(
        queries, out_grad, nbr_states, key_weight, value_weight,
        q_gain.reshape(1, -1), k_gain.reshape(1, -1), jnp.asarray(cos), jnp.asarray(sin),
        nbr_owner, nbr_slot,
    )


def solution(mesh):
    in_specs = (
        P("ctx", "enc"),
        P("ctx", "enc"),
        P("ctx", None, "enc"),
        P("ctx", "enc"),
        P("ctx", "enc"),
        P("enc"),
        P("enc"),
        P(),
        P(),
    )
    out_specs = (P("ctx", "enc"), P("ctx", None, "enc"))
    return jax.shard_map(shards, mesh=mesh, in_specs=in_specs, out_specs=out_specs, check_vma=False)
```

```python
import functools

import jax
import jax.numpy as jnp
import numpy as np
from jax import lax
from jax.experimental import pallas as pl
from jax.experimental.pallas import tpu as pltpu
from jax.sharding import PartitionSpec as P

MESH = pl.DeviceIdType.MESH
F32 = jnp.float32
BF16 = jnp.bfloat16

DH = 128
SPAN = 64
NT = 128
EPSILON = 1e-06
LOG_BASE = 9.210340371976184
SCALE = DH**-0.5
CHUNKS = 4
CW = 256

NT_DIMS = (((1,), (1,)), ((), ()))
TN_DIMS = (((0,), (0,)), ((), ()))


def rope_tables():
    half = DH // 2
    freq = np.exp(np.arange(half) * (-2.0 * LOG_BASE / DH))
    angle = np.arange(NT)[:, None] * freq[None, :]
    cos = np.concatenate([np.cos(angle)] * 2, axis=1)
    sin = np.concatenate([-np.sin(angle), np.sin(angle)], axis=1)
    twice = lambda t: np.concatenate([t, t], axis=0).astype(np.float32)
    return twice(cos), twice(sin)


def swap(v):
    return pltpu.roll(v, DH // 2, 1)


def unit(v):
    r = lax.rsqrt(jnp.mean(v * v, axis=1, keepdims=True) + EPSILON)
    return v * r, r


def rope(v, cos, sin):
    return v * cos + swap(v) * sin


def rope_back(d, cos, sin):
    return d * cos + swap(d * sin)


def unit_back(d, xhat, r):
    return r * (d - xhat * jnp.mean(d * xhat, axis=1, keepdims=True))


def kernel(
    q_hbm, do_hbm, pool_hbm, kw_hbm, vw_hbm, qg_hbm, kg_hbm, cos_hbm, sin_hbm, owner_ref, slot_ref,
    qgrad_hbm, sgrad_hbm,
    q_ref, do_ref, qg_ref, kg_ref, cos_ref, sin_ref, qgrad_ref, sgrad_ref,
    pool_lo, pool_hi, kw_all, vw_all, ebuf, halo, qwin, qbd, dobd, dqwin, qback_out, qback, dkv, kps, vps,
    acc, sib_out, sib_in, t_out, t_in, m_out, m_in, refg, ret_out, ret_in, stab,
    in_s, out_s, ag_s, ag_r, e_s, e_r, sib_s, sib_r, h_s, h_r, rs_s, rs_r, a2a_s, a2a_r,
):
    c, e = lax.axis_index("ctx"), lax.axis_index("enc")
    z, x = c // 4, c % 4
    y, core = e // 2, e % 2
    up, dn, opp = (y + 1) % 4, (y + 3) % 4, (y + 2) % 4
    enc = lambda y_, core_: y_ * 2 + core_
    other = (c, enc(y, 1 - core))
    pool_all = (pool_lo, pool_hi)
    pending = []

    def send(src, dst, ssem, rsem, dev):
        cp = pltpu.make_async_remote_copy(
            src_ref=src, dst_ref=dst, send_sem=ssem, recv_sem=rsem, device_id=dev, device_id_type=MESH
        )
        cp.start()
        pending.append(cp)
        return cp

    loads = []

    def load(src, dst):
        cp = pltpu.make_async_copy(src, dst, in_s.at[len(loads)])
        cp.start()
        loads.append(cp)
        return cp

    in_pool = [load(pool_hbm.at[:, :, pl.ds(128 * f, 128)], pool_all[f].at[z, x]) for f in range(2)]
    in_q = [load(q_hbm, q_ref), load(do_hbm, do_ref)]
    in_w = [
        [load(src.at[:, pl.ds(j * CW, CW)], dst.at[j, z, x]) for src, dst in ((kw_hbm, kw_all), (vw_hbm, vw_all))]
        for j in range(CHUNKS)
    ]
    in_small = [
        load(src, dst) for src, dst in ((qg_hbm, qg_ref), (kg_hbm, kg_ref), (cos_hbm, cos_ref), (sin_hbm, sin_ref))
    ]

    barrier = pltpu.get_barrier_semaphore()
    for d in range(1, 16):
        pl.semaphore_signal(barrier, inc=1, device_id=((c + d) % 16, e), device_id_type=MESH)
    for there in (enc(up, core), enc(dn, core), enc(y, 1 - core)):
        pl.semaphore_signal(barrier, inc=1, device_id=(c, there), device_id_type=MESH)
    pl.semaphore_wait(barrier, 18)

    class Item:
        def __init__(self, n, bufs, blocks=None):
            self.n, self.bufs, self.blocks = n, bufs, blocks
            self.cp = {}

        def view(self, ab, first, second):
            zi, xi = (second, first) if ab == 0 else (first, second)
            ref = self.bufs[ab]
            return ref.at[zi, xi] if self.blocks is None else ref.at[zi, xi, self.blocks[ab]]

        def half(self, ab, first, second, h):
            zi, xi = (second, first) if ab == 0 else (first, second)
            part = pl.ds(64 * h, 64) if self.blocks is None else pl.ds(self.blocks[ab].start + h, 1)
            return self.bufs[ab].at[zi, xi, part]

        def coords(self, ab):
            return (x, z) if ab == 0 else (z, x)

        def dev(self, ab, first, second):
            return (second * 4 + first, e) if ab == 0 else (first * 4 + second, e)

        def go(self, step, ab, d, ref, to):
            self.cp[step, ab, d] = send(
                ref, ref, ag_s.at[self.n, ab, step, d], ag_r.at[self.n, ab, step, d], to
            )

        def s1(self):
            for ab in (0, 1):
                f, s = self.coords(ab)
                for d in (0, 1):
                    self.go(0, ab, d, self.view(ab, f, s), self.dev(ab, (f + (1, 3)[d]) % 4, s))

        def s2(self):
            for ab in (0, 1):
                f, s = self.coords(ab)
                for d in (0, 1):
                    self.cp[0, ab, d].wait_recv()
                    to = self.dev(ab, (f + (1, 3)[d]) % 4, s)
                    self.go(1, ab, d, self.half(ab, (f + (3, 1)[d]) % 4, s, d), to)

        def s3(self):
            for ab in (0, 1):
                f, s = self.coords(ab)
                for d in (0, 1):
                    self.cp[1, ab, d].wait_recv()
                for d in (0, 1):
                    to = self.dev(ab, f, (s + (1, 3)[d]) % 4)
                    self.go(2, ab, d, self.view(ab, pl.ds(0, 4), s), to)

        def s4(self):
            for ab in (0, 1):
                f, s = self.coords(ab)
                for d in (0, 1):
                    self.cp[2, ab, d].wait_recv()
                    to = self.dev(ab, f, (s + (1, 3)[d]) % 4)
                    self.go(3, ab, d, self.view(ab, pl.ds(2 * d, 2), (s + (3, 1)[d]) % 4), to)

        def done(self):
            for ab in (0, 1):
                for d in (0, 1):
                    self.cp[3, ab, d].wait_recv()

    stored = (pl.ds(0, 2), pl.ds(2, 2))
    pool = [Item(f, (pool_all[f], pool_all[f]), stored) for f in range(2)]
    w = [Item(2 + j, (kw_all.at[j], vw_all.at[j])) for j in range(CHUNKS)]

    for f in range(2):
        in_pool[f].wait()
        pool[f].s1()
    for cp in in_w[0]:
        cp.wait()
    w[0].s1()
    for cp in in_q:
        cp.wait()
    halo_cps = [
        send(src.at[pl.ds(0, SPAN)], halo.at[i], h_s.at[i], h_r.at[i], ((c + 15) % 16, e))
        for i, src in enumerate((q_ref, do_ref))
    ]
    pool[0].s2()
    for pair in in_w[1:]:
        for cp in pair:
            cp.wait()
    w[2].s1()
    pool[1].s2()
    pool[0].s3()
    pool[1].s3()
    w[3].s1()
    w[0].s2()
    w[1].s1()
    for cp in in_small:
        cp.wait()

    def table(p, _):
        first, last, count = jnp.int32(0), jnp.int32(0), jnp.int32(0)
        r_first, r_last, r_count = jnp.int32(0), jnp.int32(0), jnp.int32(0)
        for r in range(8):
            hit = owner_ref[r % 2, c * 4 + r // 2] == p
            first = jnp.where(hit & (count == 0), r, first)
            last = jnp.where(hit, r, last)
            count = count + hit.astype(jnp.int32)
            there = owner_ref[r % 2, p * 4 + r // 2] == c
            n = slot_ref[r % 2, p * 4 + r // 2]
            r_first = jnp.where(there & (r_count == 0), n, r_first)
            r_last = jnp.where(there, n, r_last)
            r_count = r_count + there.astype(jnp.int32)
        stab[0, p], stab[1, p], stab[2, p] = first, last, count
        stab[3, p] = jnp.where(r_count > 0, r_first, -1)
        stab[4, p] = jnp.where(r_count > 1, r_last, -1)
        return 0

    lax.fori_loop(0, 16, table, 0)

    for cp in halo_cps:
        cp.wait_recv()
    keep = jnp.where(c == 15, 0.0, 1.0)
    first_row = lax.broadcasted_iota(jnp.int32, (4 * SPAN, DH), 0) == 0

    def windows(ref, which, cols):
        own_rows = ref[:, cols].astype(F32)
        nxt = halo[which, :, cols].astype(F32) * keep
        shifted = pltpu.roll(jnp.concatenate([own_rows[SPAN:], nxt], axis=0), 1, 0)
        return jnp.where(first_row, own_rows[SPAN - 1 : SPAN], shifted)

    qcos = jnp.concatenate([cos_ref[0:SPAN, :]] * 4, axis=0)
    qsin = jnp.concatenate([sin_ref[0:SPAN, :]] * 4, axis=0)
    zero = jnp.zeros((SPAN, DH), BF16)

    def prepare(h):
        j, hh = h // 2, h % 2
        cols = pl.ds(h * DH, DH)
        v = windows(q_ref, 0, cols)
        qwin[h] = v
        xhat, _ = unit(v)
        rot = (rope(xhat * qg_ref[:, cols], qcos, qsin) * SCALE).astype(BF16)
        dov = windows(do_ref, 1, cols).astype(BF16)
        for s in range(4):
            r = slice(s * SPAN, (s + 1) * SPAN)
            mine = slice(hh * DH, (hh + 1) * DH)
            rest = slice((1 - hh) * DH, (2 - hh) * DH)
            rows = slice(hh * SPAN, (hh + 1) * SPAN)
            qbd[j, s, rows, mine] = rot[r]
            qbd[j, s, rows, rest] = zero
            dobd[j, s, rows, mine] = dov[r]
            dobd[j, s, rows, rest] = zero

    for h in range(8):
        prepare(h)
    pool[0].s4()

    ring, sib = {}, {}

    def to_sibling(f, i, slot):
        ref = ebuf.at[f, slot]
        sib[f, i] = send(ref, ref, sib_s.at[f, i], sib_r.at[f, i], other)

    def y1(f):
        for r in range(8):
            o, n = owner_ref[r % 2, c * 4 + r // 2], slot_ref[r % 2, c * 4 + r // 2]
            ebuf[f, e, r * NT : (r + 1) * NT, :] = pool_all[f][o // 4, o % 4, n]
        for d, to in ((0, up), (1, dn)):
            ref = ebuf.at[f, e]
            ring[f, 0, d] = send(ref, ref, e_s.at[f, 0, d], e_r.at[f, 0, d], (c, enc(to, core)))
        to_sibling(f, 0, e)

    def y2(f):
        for d, frm, to in ((0, dn, up), (1, up, dn)):
            ring[f, 0, d].wait_recv()
            slot = enc(frm, core)
            part = ebuf.at[f, slot, pl.ds(512 * d, 512)]
            ring[f, 1, d] = send(part, part, e_s.at[f, 1, d], e_r.at[f, 1, d], (c, enc(to, core)))
            to_sibling(f, 1 + d, slot)

    def y3(f):
        for d in (0, 1):
            ring[f, 1, d].wait_recv()
        to_sibling(f, 3, enc(opp, core))

    pool[1].s4()
    w[0].s3()
    pool[0].done()
    y1(0)
    w[1].s2()
    w[3].s2()
    w[2].s2()
    pool[1].done()
    y1(1)
    w[0].s4()
    w[1].s3()
    y2(0)
    w[2].s3()
    y2(1)
    y3(0)
    y3(1)
    w[0].done()
    for f in range(2):
        for i in range(4):
            sib[f, i].wait_recv()

    def project(j, s):
        rows = slice(s * 256, (s + 1) * 256)
        ecat = jnp.concatenate([ebuf[f, i, rows, :] for i in range(8) for f in range(2)], axis=1)
        kw, vw = kw_all[j].reshape(2048, CW), vw_all[j].reshape(2048, CW)
        kps[s % 2] = jnp.dot(ecat, kw, preferred_element_type=F32).astype(BF16).astype(F32)
        vps[s % 2] = jnp.dot(ecat, vw, preferred_element_type=F32).astype(BF16)

    def keep_rows(s, cols, v):
        for rr in range(2):
            for h in range(2):
                to = h * 512 + (2 * s + rr) * 64
                dkv[to : to + 64, cols] = v[rr * NT + h * 64 : rr * NT + h * 64 + 64]

    def attend(j, s):
        rows = slice(s * 256, (s + 1) * 256)
        kp, vp = kps[s % 2], vps[s % 2]
        cos, sin = cos_ref[...], sin_ref[...]
        hats, rs, gains, ks = [], [], [], []
        for hh in range(2):
            xhat, r = unit(kp[:, hh * DH : (hh + 1) * DH])
            g = kg_ref[:, (2 * j + hh) * DH : (2 * j + hh + 1) * DH]
            ks.append(rope(xhat * g, cos, sin).astype(BF16))
            hats.append(xhat)
            rs.append(r)
            gains.append(g)
        k = jnp.concatenate(ks, axis=1)
        qb, dob = qbd[j, s], dobd[j, s]
        scores = lax.dot_general(k, qb, NT_DIMS, preferred_element_type=F32)
        dp = lax.dot_general(vp, dob, NT_DIMS, preferred_element_type=F32)
        p = jnp.exp(scores)
        p = p * (1.0 / jnp.sum(p, axis=0, keepdims=True))
        ds = (p * (dp - jnp.sum(p * dp, axis=0, keepdims=True))).astype(BF16)
        dv = jnp.dot(p.astype(BF16), dob, preferred_element_type=F32)
        dk = jnp.dot(ds, qb, preferred_element_type=F32)
        dq = lax.dot_general(ds, k, TN_DIMS, preferred_element_type=F32) * SCALE
        for hh in range(2):
            cols = slice(hh * DH, (hh + 1) * DH)
            d = rope_back(dk[:, cols], cos, sin) * gains[hh]
            keep_rows(s, cols, unit_back(d, hats[hh], rs[hh]).astype(BF16))
        keep_rows(s, slice(CW, 2 * CW), dv.astype(BF16))
        qrows = slice(s * SPAN, (s + 1) * SPAN)
        for hh in range(2):
            h = 2 * j + hh
            xhat, r = unit(qwin[h, qrows, :])
            d = dq[hh * SPAN : (hh + 1) * SPAN, hh * DH : (hh + 1) * DH]
            d = rope_back(d, cos_ref[0:SPAN, :], sin_ref[0:SPAN, :]) * qg_ref[:, h * DH : (h + 1) * DH]
            dqwin[qrows, h * DH : (h + 1) * DH] = unit_back(d, xhat, r)

    def compute(j, part):
        if part == 0:
            project(j, 0)
        for s in (2 * part, 2 * part + 1):
            if s < 3:
                project(j, s + 1)
            attend(j, s)

    def product(j, f, which):
        xi = 2 * (core if which else 1 - core) + f
        for i in range(2):
            wcat = jnp.concatenate([b[j, 2 * i : 2 * i + 2, xi].reshape(256, CW) for b in (kw_all, vw_all)], axis=1)
            part = lax.dot_general(dkv[...], wcat, NT_DIMS, preferred_element_type=F32)
            for k in range(2):
                new = part[:, k * 128 : (k + 1) * 128]
                if j > 0:
                    new = new + acc[f, which, 2 * i + k]
                if j == CHUNKS - 1 and which == 0:
                    sib_out[f, 2 * i + k] = new.astype(BF16)
                else:
                    acc[f, which, 2 * i + k] = new

    def products(j):
        for f in range(2):
            for which in range(2):
                product(j, f, which)

    def query_rows(j):
        for h in (2 * j, 2 * j + 1):
            cols = slice(h * DH, (h + 1) * DH)
            back = pltpu.roll(dqwin[:, cols], 4 * SPAN - 1, 0).astype(BF16)
            qgrad_ref[SPAN:, cols] = back[: 3 * SPAN]
            qback_out[:, cols] = back[3 * SPAN :]

    compute(0, 0)
    w[1].s4()
    compute(0, 1)
    w[2].s4()
    products(0)
    w[3].s3()
    w[1].done()
    compute(1, 0)
    compute(1, 1)
    products(1)
    query_rows(0)
    query_rows(1)
    w[2].done()
    compute(2, 0)
    w[3].s4()
    compute(2, 1)
    products(2)
    query_rows(2)
    w[3].done()
    compute(3, 0)
    compute(3, 1)

    rs_cp = {}

    def rs_send(p, k, src, dst, to):
        rs_cp[p, k] = send(src, dst, rs_s.at[p, k], rs_r.at[p, k], to)

    def rs_a(f):
        product(CHUNKS - 1, f, 0)
        for h in range(2):
            rows = pl.ds(512 * h, 512)
            rs_send(2 * f + h, 0, sib_out.at[f, :, rows], sib_in.at[f, :, rows], other)
        product(CHUNKS - 1, f, 1)

    def both(p, i, start, size):
        rows = pl.ds(512 * (p % 2) + start, size)
        return acc[p // 2, 1, i, rows, :] + sib_in[p // 2, i, rows, :].astype(F32)

    sides = ((0, up), (1, dn))

    def rs_b(p):
        rs_cp[p, 0].wait_recv()
        for d, to in sides:
            t_out[p, d] = both(p, opp, 256 * d, 256).astype(BF16)
            rs_send(p, 1 + d, t_out.at[p, d], t_in.at[p, d], (c, enc(to, core)))
        for d, to in sides:
            m_out[p, d, 1 - d] = both(p, to, 256 * (1 - d), 256).astype(BF16)
            rs_send(p, 3 + d, m_out.at[p, d, 1 - d], m_in.at[p, d, 1 - d], (c, enc(to, core)))

    def rs_c(p):
        for d, to in sides:
            mine = both(p, to, 256 * d, 256)
            rs_cp[p, 1 + d].wait_recv()
            m_out[p, d, d] = (mine + t_in[p, d].astype(F32)).astype(BF16)
            rs_send(p, 5 + d, m_out.at[p, d, d], m_in.at[p, d, d], (c, enc(to, core)))

    def rs_d(p):
        for k in range(3, 7):
            rs_cp[p, k].wait_recv()
        for h in range(2):
            total = both(p, y, 256 * h, 256) + m_in[p, 0, h].astype(F32) + m_in[p, 1, h].astype(F32)
            refg[p, 4 * h : 4 * h + 4] = total.reshape(4, 64, 128)
        for d in range(16):
            to = (c + d) % 16
            count = stab[2, to]
            one = jnp.where(count > 0, 1.0, 0.0)
            two = jnp.where(count > 1, 1.0, 0.0)
            block0 = (refg[p, stab[0, to]] * one).astype(BF16)
            block1 = (refg[p, stab[1, to]] * two).astype(BF16)
            if d == 0:
                ret_in[p, c, 0] = block0
                ret_in[p, c, 1] = block1
                continue
            ret_out[p, d, 0] = block0
            ret_out[p, d, 1] = block1
            rs_cp[p, 7, d] = send(
                ret_out.at[p, d], ret_in.at[p, c], a2a_s.at[p, d], a2a_r.at[p, d], (to, e)
            )

    outs = []

    def store(src, dst):
        cp = pltpu.make_async_copy(src, dst, out_s.at[len(outs)])
        cp.start()
        outs.append(cp)

    def rs_e(p):
        for d in range(1, 16):
            rs_cp[p, 7, d].wait_recv()

        def add(o, sums):
            b0, b1 = ret_in[p, o, 0].astype(F32), ret_in[p, o, 1].astype(F32)
            n0, n1 = stab[3, o], stab[4, o]
            return tuple(
                a + b0 * jnp.where(n0 == n, 1.0, 0.0) + b1 * jnp.where(n1 == n, 1.0, 0.0)
                for n, a in enumerate(sums)
            )

        for n, a in enumerate(lax.fori_loop(0, 16, add, tuple(jnp.zeros((64, 128), F32) for _ in range(4)))):
            sgrad_ref[p, n] = a
        store(sgrad_ref.at[p], sgrad_hbm.at[:, pl.ds(64 * (p % 2), 64), pl.ds(128 * (p // 2), 128)])

    rs_a(0)
    rs_b(0)
    query_rows(3)
    qback_cp = send(qback_out, qback, h_s.at[2], h_r.at[2], ((c + 1) % 16, e))
    rs_c(0)
    rs_b(1)
    rs_d(0)
    rs_c(1)
    rs_a(1)
    rs_d(1)
    rs_b(2)
    rs_c(2)
    rs_b(3)
    store(qgrad_ref.at[pl.ds(SPAN, 3 * SPAN)], qgrad_hbm.at[pl.ds(SPAN, 3 * SPAN)])
    rs_d(2)
    rs_c(3)
    rs_d(3)

    qback_cp.wait_recv()
    live = jnp.where(c == 0, 0.0, 1.0)
    last_row = lax.broadcasted_iota(jnp.int32, (SPAN, DH), 0) == SPAN - 1
    for h in range(8):
        cols = slice(h * DH, (h + 1) * DH)
        head = qback[:, cols].astype(F32) * live
        qgrad_ref[0:SPAN, cols] = jnp.where(last_row, dqwin[0:1, cols], head).astype(BF16)
    store(qgrad_ref.at[pl.ds(0, SPAN)], qgrad_hbm.at[pl.ds(0, SPAN)])

    for p in range(4):
        rs_e(p)
    for cp in outs:
        cp.wait()
    for cp in pending:
        cp.wait_send()


def shards(queries, out_grad, nbr_states, key_weight, value_weight, q_gain, k_gain, nbr_owner, nbr_slot):
    cos, sin = rope_tables()
    hbm = pl.BlockSpec(memory_space=pl.ANY)
    smem = pl.BlockSpec(memory_space=pltpu.SMEM)
    dma = pltpu.SemaphoreType.DMA
    vmem = pltpu.VMEM
    return pl.pallas_call(
        kernel,
        out_shape=(
            jax.ShapeDtypeStruct((256, 1024), BF16),
            jax.ShapeDtypeStruct((4, NT, 256), F32),
        ),
        in_specs=[hbm] * 9 + [smem] * 2,
        out_specs=(hbm, hbm),
        scratch_shapes=[
            vmem((256, 1024), BF16),
            vmem((256, 1024), BF16),
            vmem((1, 1024), F32),
            vmem((1, 1024), F32),
            vmem((256, DH), F32),
            vmem((256, DH), F32),
            vmem((256, 1024), BF16),
            vmem((4, 4, 64, 128), F32),
            vmem((4, 4, 4, NT, 128), BF16),
            vmem((4, 4, 4, NT, 128), BF16),
            vmem((CHUNKS, 4, 4, 128, CW), BF16),
            vmem((CHUNKS, 4, 4, 128, CW), BF16),
            vmem((2, 8, 1024, 128), BF16),
            vmem((2, SPAN, 1024), BF16),
            vmem((8, 4 * SPAN, DH), F32),
            vmem((4, 4, 2 * SPAN, 256), BF16),
            vmem((4, 4, 2 * SPAN, 256), BF16),
            vmem((4 * SPAN, 1024), F32),
            vmem((SPAN, 1024), BF16),
            vmem((SPAN, 1024), BF16),
            vmem((1024, 2 * CW), BF16),
            vmem((2, 256, CW), F32),
            vmem((2, 256, CW), BF16),
            vmem((2, 2, 4, 1024, 128), F32),
            vmem((2, 4, 1024, 128), BF16),
            vmem((2, 4, 1024, 128), BF16),
            vmem((4, 2, 256, 128), BF16),
            vmem((4, 2, 256, 128), BF16),
            vmem((4, 2, 2, 256, 128), BF16),
            vmem((4, 2, 2, 256, 128), BF16),
            vmem((4, 8, 64, 128), F32),
            vmem((4, 16, 2, 64, 128), BF16),
            vmem((4, 16, 2, 64, 128), BF16),
            pltpu.SMEM((5, 16), jnp.int32),
            dma((16,)),
            dma((6,)),
            dma((2 + CHUNKS, 2, 4, 2)),
            dma((2 + CHUNKS, 2, 4, 2)),
            dma((2, 2, 2)),
            dma((2, 2, 2)),
            dma((2, 4)),
            dma((2, 4)),
            dma((3,)),
            dma((3,)),
            dma((4, 7)),
            dma((4, 7)),
            dma((4, 16)),
            dma((4, 16)),
        ],
        compiler_params=pltpu.CompilerParams(
            collective_id=0, has_side_effects=True, vmem_limit_bytes=60 * 2**20
        ),
    )(
        queries, out_grad, nbr_states, key_weight, value_weight,
        q_gain.reshape(1, -1), k_gain.reshape(1, -1), jnp.asarray(cos), jnp.asarray(sin),
        nbr_owner.T, nbr_slot.T,
    )


def solution(mesh):
    in_specs = (
        P("ctx", "enc"),
        P("ctx", "enc"),
        P("ctx", None, "enc"),
        P("ctx", "enc"),
        P("ctx", "enc"),
        P("enc"),
        P("enc"),
        P(),
        P(),
    )
    out_specs = (P("ctx", "enc"), P("ctx", None, "enc"))
    return jax.shard_map(shards, mesh=mesh, in_specs=in_specs, out_specs=out_specs, check_vma=False)
```

```python
import functools

import jax
import jax.numpy as jnp
import numpy as np
from jax import lax
from jax.experimental import pallas as pl
from jax.experimental.pallas import tpu as pltpu
from jax.sharding import PartitionSpec as P

MESH = pl.DeviceIdType.MESH
F32 = jnp.float32
BF16 = jnp.bfloat16

DH = 128
SPAN = 64
NT = 128
EPSILON = 1e-06
LOG_BASE = 9.210340371976184
SCALE = DH**-0.5
CHUNKS = 4
CW = 256

NT_DIMS = (((1,), (1,)), ((), ()))
TN_DIMS = (((0,), (0,)), ((), ()))


def rope_tables():
    half = DH // 2
    freq = np.exp(np.arange(half) * (-2.0 * LOG_BASE / DH))
    angle = np.arange(NT)[:, None] * freq[None, :]
    cos = np.concatenate([np.cos(angle)] * 2, axis=1)
    sin = np.concatenate([-np.sin(angle), np.sin(angle)], axis=1)
    twice = lambda t: np.concatenate([t, t], axis=0).astype(np.float32)
    return twice(cos), twice(sin)


def swap(v):
    return pltpu.roll(v, DH // 2, 1)


def unit(v):
    r = lax.rsqrt(jnp.mean(v * v, axis=1, keepdims=True) + EPSILON)
    return v * r, r


def rope(v, cos, sin):
    return v * cos + swap(v) * sin


def rope_back(d, cos, sin):
    return d * cos + swap(d * sin)


def unit_back(d, xhat, r):
    return r * (d - xhat * jnp.mean(d * xhat, axis=1, keepdims=True))


def kernel(
    q_hbm, do_hbm, pool_hbm, kw_hbm, vw_hbm, qg_hbm, kg_hbm, cos_hbm, sin_hbm, owner_hbm, slot_hbm,
    qgrad_hbm, sgrad_hbm,
    q_ref, do_ref, qg_ref, kg_ref, cos_ref, sin_ref, qgrad_ref, sgrad_ref,
    line, gt_out, gt_in, gm_out, gm_in, kw_all, vw_all, ebuf, halo, qwin, qbd, dobd, dqwin, qback_out, qback, dkv, kps, vps,
    acc, sib_out, sib_in, t_out, t_in, m_out, m_in, refg, ret_out, ret_in, stab, owner_ref, slot_ref,
    in_s, out_s, w_s, w_r, g_s, g_r, e_s, e_r, h_s, h_r, rs_s, rs_r, ret_s, ret_r,
):
    c, e = lax.axis_index("ctx"), lax.axis_index("enc")
    z, x = c // 4, c % 4
    y, core = e // 2, e % 2
    up, dn, opp = (y + 1) % 4, (y + 3) % 4, (y + 2) % 4
    enc = lambda y_, core_: y_ * 2 + core_
    other = (c, enc(y, 1 - core))

    def descriptor(src, dst, ssem, rsem, dev):
        return pltpu.make_async_remote_copy(
            src_ref=src, dst_ref=dst, send_sem=ssem, recv_sem=rsem, device_id=dev, device_id_type=MESH
        )

    def send(src, dst, ssem, rsem, dev):
        descriptor(src, dst, ssem, rsem, dev).start()

    def landed(ref, sem):
        descriptor(ref, ref, sem, sem, other).wait_recv()

    def sent(ref, sem):
        descriptor(ref, ref, sem, sem, other).wait_send()

    def load(src, dst, i):
        cp = pltpu.make_async_copy(src, dst, in_s.at[i])
        cp.start()
        return cp

    in_pool = [
        load(pool_hbm.at[:, :, pl.ds(128 * f, 128)], line.at[f, (x, z)[f]], f) for f in range(2)
    ]
    in_small = [load(owner_hbm, owner_ref, 2), load(slot_hbm, slot_ref, 3)]
    in_w = [
        [load(src.at[:, pl.ds(j * CW, CW)], dst.at[j, z, x], 4 + 2 * j + i) for i, (src, dst) in enumerate(((kw_hbm, kw_all), (vw_hbm, vw_all)))]
        for j in range(CHUNKS)
    ]
    in_q = [load(q_hbm, q_ref, 12), load(do_hbm, do_ref, 13)]
    in_small += [
        load(src, dst, 14 + i)
        for i, (src, dst) in enumerate(((qg_hbm, qg_ref), (kg_hbm, kg_ref), (cos_hbm, cos_ref), (sin_hbm, sin_ref)))
    ]

    barrier = pltpu.get_barrier_semaphore()
    for d in range(1, 16):
        pl.semaphore_signal(barrier, inc=1, device_id=((c + d) % 16, e), device_id_type=MESH)
    for there in (enc(up, core), enc(dn, core), enc(y, 1 - core)):
        pl.semaphore_signal(barrier, inc=1, device_id=(c, there), device_id_type=MESH)
    pl.semaphore_wait(barrier, 18)

    class Chunk:
        def __init__(self, j):
            self.j = j

        def view(self, ab, first, second):
            zi, xi = (second, first) if ab == 0 else (first, second)
            return (kw_all, vw_all)[ab].at[self.j, zi, xi]

        def half(self, ab, first, second, h):
            zi, xi = (second, first) if ab == 0 else (first, second)
            return (kw_all, vw_all)[ab].at[self.j, zi, xi, pl.ds(64 * h, 64)]

        def coords(self, ab):
            return (x, z) if ab == 0 else (z, x)

        def dev(self, ab, first, second):
            return (second * 4 + first, e) if ab == 0 else (first * 4 + second, e)

        def go(self, step, ref, to):
            send(ref, ref, w_s.at[step], w_r.at[self.j, step], to)

        def got(self, step):
            block = kw_all.at[self.j]
            landed((block.at[0], block.at[0, pl.ds(0, 2)], block, block.at[pl.ds(0, 2)])[step], w_r.at[self.j, step])

        def s1(self):
            for ab in (0, 1):
                f, s = self.coords(ab)
                for d in (0, 1):
                    self.go(0, self.view(ab, f, s), self.dev(ab, (f + (1, 3)[d]) % 4, s))

        def s2(self):
            self.got(0)
            for ab in (0, 1):
                f, s = self.coords(ab)
                for d in (0, 1):
                    to = self.dev(ab, (f + (1, 3)[d]) % 4, s)
                    self.go(1, self.half(ab, (f + (3, 1)[d]) % 4, s, d), to)

        def s3(self):
            self.got(1)
            for ab in (0, 1):
                f, s = self.coords(ab)
                for d in (0, 1):
                    self.go(2, self.view(ab, pl.ds(0, 4), s), self.dev(ab, f, (s + (1, 3)[d]) % 4))

        def s4(self):
            self.got(2)
            for ab in (0, 1):
                f, s = self.coords(ab)
                for d in (0, 1):
                    to = self.dev(ab, f, (s + (1, 3)[d]) % 4)
                    self.go(3, self.view(ab, pl.ds(2 * d, 2), (s + (3, 1)[d]) % 4), to)

        def done(self):
            self.got(3)

    def ahead(f, first, second):
        return (second * 4 + first, e) if f == 0 else (first * 4 + second, e)

    def referred(f, second, r):
        to = ahead(f, (x, z)[f], second)[0]
        o, n = owner_ref[r % 2, to * 4 + r // 2], slot_ref[r % 2, to * 4 + r // 2]
        first, there = (o % 4, o // 4) if f == 0 else (o // 4, o % 4)
        block = line[f, first, n]
        return jnp.where(there == (z, x)[f], block, jnp.zeros_like(block))

    def pool1():
        for f in range(2):
            a, b = ((x, z), (z, x))[f]
            for d in (0, 1):
                ref = line.at[f, a]
                send(ref, ref, g_s.at[0], g_r.at[0], ahead(f, (a + (1, 3)[d]) % 4, b))

    def pool2():
        landed(line.at[0], g_r.at[0])
        for f in range(2):
            a, b = ((x, z), (z, x))[f]
            for d in (0, 1):
                ref = line.at[f, (a + (3, 1)[d]) % 4, pl.ds(2 * d, 2)]
                send(ref, ref, g_s.at[1], g_r.at[1], ahead(f, (a + (1, 3)[d]) % 4, b))

    def pool3():
        landed(line.at[0, pl.ds(0, 2)], g_r.at[1])
        for f in range(2):
            a, b = ((x, z), (z, x))[f]
            for d in (0, 1):
                for r in range(4):
                    gt_out[f, d, r] = referred(f, (b + 2) % 4, 4 * d + r)
                send(gt_out.at[f, d], gt_in.at[f, d], g_s.at[2], g_r.at[2], ahead(f, a, (b + (1, 3)[d]) % 4))
        for f in range(2):
            a, b = ((x, z), (z, x))[f]
            for d in (0, 1):
                to = (b + (1, 3)[d]) % 4
                part = pl.ds(4 * (1 - d), 4)
                for r in range(4):
                    gm_out[f, d, 4 * (1 - d) + r] = referred(f, to, 4 * (1 - d) + r)
                send(gm_out.at[f, d, part], gm_in.at[f, d, part], g_s.at[3], g_r.at[3], ahead(f, a, to))

    def pool4():
        landed(gt_in, g_r.at[2])
        for f in range(2):
            a, b = ((x, z), (z, x))[f]
            for d in (0, 1):
                to = (b + (1, 3)[d]) % 4
                part = pl.ds(4 * d, 4)
                for r in range(4):
                    gm_out[f, d, 4 * d + r] = referred(f, to, 4 * d + r) + gt_in[f, d, r]
                send(gm_out.at[f, d, part], gm_in.at[f, d, part], g_s.at[3], g_r.at[3], ahead(f, a, to))

    w = [Chunk(j) for j in range(CHUNKS)]

    for cp in in_pool:
        cp.wait()
    pool1()
    for cp in in_w[0]:
        cp.wait()
    w[0].s1()
    for cp in in_q:
        cp.wait()
    for i, src in enumerate((q_ref, do_ref)):
        send(src.at[pl.ds(0, SPAN)], halo.at[i], h_s.at[0], h_r.at[0], ((c + 15) % 16, e))
    pool2()
    for pair in in_w[1:]:
        for cp in pair:
            cp.wait()
    for cp in in_small:
        cp.wait()
    w[0].s2()
    w[1].s1()
    pool3()

    def table(p, _):
        first, last, count = jnp.int32(0), jnp.int32(0), jnp.int32(0)
        r_first, r_last, r_count = jnp.int32(0), jnp.int32(0), jnp.int32(0)
        for r in range(8):
            hit = owner_ref[r % 2, c * 4 + r // 2] == p
            first = jnp.where(hit & (count == 0), r, first)
            last = jnp.where(hit, r, last)
            count = count + hit.astype(jnp.int32)
            there = owner_ref[r % 2, p * 4 + r // 2] == c
            n = slot_ref[r % 2, p * 4 + r // 2]
            r_first = jnp.where(there & (r_count == 0), n, r_first)
            r_last = jnp.where(there, n, r_last)
            r_count = r_count + there.astype(jnp.int32)
        stab[0, p], stab[1, p], stab[2, p] = first, last, count
        stab[3, p] = jnp.where(r_count > 0, r_first, -1)
        stab[4, p] = jnp.where(r_count > 1, r_last, -1)
        return 0

    lax.fori_loop(0, 16, table, 0)

    landed(halo, h_r.at[0])
    keep = jnp.where(c == 15, 0.0, 1.0)
    first_row = lax.broadcasted_iota(jnp.int32, (4 * SPAN, DH), 0) == 0

    def windows(ref, which, cols):
        own_rows = ref[:, cols].astype(F32)
        nxt = halo[which, :, cols].astype(F32) * keep
        shifted = pltpu.roll(jnp.concatenate([own_rows[SPAN:], nxt], axis=0), 1, 0)
        return jnp.where(first_row, own_rows[SPAN - 1 : SPAN], shifted)

    qcos = jnp.concatenate([cos_ref[0:SPAN, :]] * 4, axis=0)
    qsin = jnp.concatenate([sin_ref[0:SPAN, :]] * 4, axis=0)
    zero = jnp.zeros((SPAN, DH), BF16)

    def prepare(h):
        j, hh = h // 2, h % 2
        cols = pl.ds(h * DH, DH)
        v = windows(q_ref, 0, cols)
        qwin[h] = v
        xhat, _ = unit(v)
        rot = (rope(xhat * qg_ref[:, cols], qcos, qsin) * SCALE).astype(BF16)
        dov = windows(do_ref, 1, cols).astype(BF16)
        for s in range(4):
            r = slice(s * SPAN, (s + 1) * SPAN)
            mine = slice(hh * DH, (hh + 1) * DH)
            rest = slice((1 - hh) * DH, (2 - hh) * DH)
            rows = slice(hh * SPAN, (hh + 1) * SPAN)
            qbd[j, s, rows, mine] = rot[r]
            qbd[j, s, rows, rest] = zero
            dobd[j, s, rows, mine] = dov[r]
            dobd[j, s, rows, rest] = zero

    for h in range(4):
        prepare(h)
    pool4()
    w[0].s3()
    for h in range(4, 8):
        prepare(h)


    def to_sibling(f, slot):
        ref = ebuf.at[f, slot]
        send(ref, ref, e_s.at[2], e_r.at[f, 2], other)

    def y1(f):
        b = (z, x)[f]
        for r in range(8):
            ebuf[f, e, r * NT : (r + 1) * NT, :] = referred(f, b, r) + gm_in[f, 0, r] + gm_in[f, 1, r]
        for to in (up, dn):
            ref = ebuf.at[f, e]
            send(ref, ref, e_s.at[0], e_r.at[f, 0], (c, enc(to, core)))
        to_sibling(f, e)

    def y2(f):
        landed(ebuf.at[f, pl.ds(0, 2)], e_r.at[f, 0])
        for d, frm, to in ((0, dn, up), (1, up, dn)):
            slot = enc(frm, core)
            part = ebuf.at[f, slot, pl.ds(512 * d, 512)]
            send(part, part, e_s.at[1], e_r.at[f, 1], (c, enc(to, core)))
            to_sibling(f, slot)

    def y3(f):
        landed(ebuf.at[f, 0], e_r.at[f, 1])
        to_sibling(f, enc(opp, core))

    landed(gm_in, g_r.at[3])
    y1(0)
    y1(1)
    w[1].s2()
    w[3].s1()
    w[2].s1()
    w[1].s3()
    w[2].s2()
    y2(0)
    w[0].s4()
    y2(1)
    w[2].s3()
    y3(0)
    y3(1)
    w[1].s4()
    w[3].s2()
    w[0].done()
    for f in range(2):
        landed(ebuf.at[f, pl.ds(0, 4)], e_r.at[f, 2])

    def project(j, s):
        rows = slice(s * 256, (s + 1) * 256)
        ecat = jnp.concatenate([ebuf[f, i, rows, :] for i in range(8) for f in range(2)], axis=1)
        kw, vw = kw_all[j].reshape(2048, CW), vw_all[j].reshape(2048, CW)
        kps[s % 2] = jnp.dot(ecat, kw, preferred_element_type=F32).astype(BF16).astype(F32)
        vps[s % 2] = jnp.dot(ecat, vw, preferred_element_type=F32).astype(BF16)

    def keep_rows(s, cols, v):
        for rr in range(2):
            for h in range(2):
                to = h * 512 + (2 * s + rr) * 64
                dkv[to : to + 64, cols] = v[rr * NT + h * 64 : rr * NT + h * 64 + 64]

    def attend(j, s):
        rows = slice(s * 256, (s + 1) * 256)
        kp, vp = kps[s % 2], vps[s % 2]
        cos, sin = cos_ref[...], sin_ref[...]
        hats, rs, gains, ks = [], [], [], []
        for hh in range(2):
            xhat, r = unit(kp[:, hh * DH : (hh + 1) * DH])
            g = kg_ref[:, (2 * j + hh) * DH : (2 * j + hh + 1) * DH]
            ks.append(rope(xhat * g, cos, sin).astype(BF16))
            hats.append(xhat)
            rs.append(r)
            gains.append(g)
        k = jnp.concatenate(ks, axis=1)
        qb, dob = qbd[j, s], dobd[j, s]
        scores = lax.dot_general(k, qb, NT_DIMS, preferred_element_type=F32)
        dp = lax.dot_general(vp, dob, NT_DIMS, preferred_element_type=F32)
        p = jnp.exp(scores)
        p = p * (1.0 / jnp.sum(p, axis=0, keepdims=True))
        ds = (p * (dp - jnp.sum(p * dp, axis=0, keepdims=True))).astype(BF16)
        dv = jnp.dot(p.astype(BF16), dob, preferred_element_type=F32)
        dk = jnp.dot(ds, qb, preferred_element_type=F32)
        dq = lax.dot_general(ds, k, TN_DIMS, preferred_element_type=F32) * SCALE
        for hh in range(2):
            cols = slice(hh * DH, (hh + 1) * DH)
            d = rope_back(dk[:, cols], cos, sin) * gains[hh]
            keep_rows(s, cols, unit_back(d, hats[hh], rs[hh]).astype(BF16))
        keep_rows(s, slice(CW, 2 * CW), dv.astype(BF16))
        qrows = slice(s * SPAN, (s + 1) * SPAN)
        for hh in range(2):
            h = 2 * j + hh
            xhat, r = unit(qwin[h, qrows, :])
            d = dq[hh * SPAN : (hh + 1) * SPAN, hh * DH : (hh + 1) * DH]
            d = rope_back(d, cos_ref[0:SPAN, :], sin_ref[0:SPAN, :]) * qg_ref[:, h * DH : (h + 1) * DH]
            dqwin[qrows, h * DH : (h + 1) * DH] = unit_back(d, xhat, r)

    def compute(j, part):
        if part == 0:
            project(j, 0)
        for s in (2 * part, 2 * part + 1):
            if s < 3:
                project(j, s + 1)
            attend(j, s)

    def product(j, f, which):
        xi = 2 * (core if which else 1 - core) + f
        for i in range(2):
            wcat = jnp.concatenate([b[j, 2 * i : 2 * i + 2, xi].reshape(256, CW) for b in (kw_all, vw_all)], axis=1)
            part = lax.dot_general(dkv[...], wcat, NT_DIMS, preferred_element_type=F32)
            for k in range(2):
                new = part[:, k * 128 : (k + 1) * 128]
                if j > 0:
                    new = new + acc[f, which, 2 * i + k]
                if j == CHUNKS - 1 and which == 0:
                    sib_out[f, 2 * i + k] = new.astype(BF16)
                else:
                    acc[f, which, 2 * i + k] = new

    def products(j):
        for f in range(2):
            for which in range(2):
                product(j, f, which)

    def query_rows(j):
        for h in (2 * j, 2 * j + 1):
            cols = slice(h * DH, (h + 1) * DH)
            back = pltpu.roll(dqwin[:, cols], 4 * SPAN - 1, 0).astype(BF16)
            qgrad_ref[SPAN:, cols] = back[: 3 * SPAN]
            qback_out[:, cols] = back[3 * SPAN :]

    compute(0, 0)
    compute(0, 1)
    w[2].s4()
    products(0)
    w[1].done()
    compute(1, 0)
    w[3].s3()
    compute(1, 1)
    products(1)
    query_rows(0)
    query_rows(1)
    w[2].done()
    compute(2, 0)
    w[3].s4()
    compute(2, 1)
    products(2)
    query_rows(2)
    w[3].done()
    compute(3, 0)
    compute(3, 1)

    def rs_send(p, k, src, dst, to):
        send(src, dst, rs_s.at[k], rs_r.at[p, k], to)

    def rs_a(f):
        product(CHUNKS - 1, f, 0)
        for h in range(2):
            rows = pl.ds(512 * h, 512)
            rs_send(2 * f + h, 0, sib_out.at[f, :, rows], sib_in.at[f, :, rows], other)
        product(CHUNKS - 1, f, 1)

    def both(p, i, start, size):
        rows = pl.ds(512 * (p % 2) + start, size)
        return acc[p // 2, 1, i, rows, :] + sib_in[p // 2, i, rows, :].astype(F32)

    sides = ((0, up), (1, dn))

    def rs_b(p):
        landed(sib_in.at[p // 2, :, pl.ds(512 * (p % 2), 512)], rs_r.at[p, 0])
        for d, to in sides:
            t_out[p, d] = both(p, opp, 256 * d, 256).astype(BF16)
            rs_send(p, 1, t_out.at[p, d], t_in.at[p, d], (c, enc(to, core)))
        for d, to in sides:
            m_out[p, d, 1 - d] = both(p, to, 256 * (1 - d), 256).astype(BF16)
            rs_send(p, 2, m_out.at[p, d, 1 - d], m_in.at[p, d, 1 - d], (c, enc(to, core)))

    def rs_c(p):
        landed(t_in.at[p], rs_r.at[p, 1])
        for d, to in sides:
            m_out[p, d, d] = (both(p, to, 256 * d, 256) + t_in[p, d].astype(F32)).astype(BF16)
            rs_send(p, 2, m_out.at[p, d, d], m_in.at[p, d, d], (c, enc(to, core)))

    def rs_d(p):
        landed(m_in.at[p], rs_r.at[p, 2])
        for h in range(2):
            total = both(p, y, 256 * h, 256) + m_in[p, 0, h].astype(F32) + m_in[p, 1, h].astype(F32)
            refg[p, 4 * h : 4 * h + 4] = total.reshape(4, 64, 128)
        for d in range(16):
            to = (c + d) % 16
            count = stab[2, to]
            one = jnp.where(count > 0, 1.0, 0.0)
            two = jnp.where(count > 1, 1.0, 0.0)
            block0 = (refg[p, stab[0, to]] * one).astype(BF16)
            block1 = (refg[p, stab[1, to]] * two).astype(BF16)
            if d == 0:
                ret_in[p, c, 0] = block0
                ret_in[p, c, 1] = block1
                continue
            ret_out[p, d, 0] = block0
            ret_out[p, d, 1] = block1
            send(ret_out.at[p, d], ret_in.at[p, c], ret_s.at[0], ret_r.at[p], (to, e))

    outs = []

    def store(src, dst):
        cp = pltpu.make_async_copy(src, dst, out_s.at[len(outs)])
        cp.start()
        outs.append(cp)

    def rs_e(p):
        landed(ret_in.at[p, pl.ds(0, 15)], ret_r.at[p])

        def add(o, sums):
            b0, b1 = ret_in[p, o, 0].astype(F32), ret_in[p, o, 1].astype(F32)
            n0, n1 = stab[3, o], stab[4, o]
            return tuple(
                a + b0 * jnp.where(n0 == n, 1.0, 0.0) + b1 * jnp.where(n1 == n, 1.0, 0.0)
                for n, a in enumerate(sums)
            )

        for n, a in enumerate(lax.fori_loop(0, 16, add, tuple(jnp.zeros((64, 128), F32) for _ in range(4)))):
            sgrad_ref[p, n] = a
        store(sgrad_ref.at[p], sgrad_hbm.at[:, pl.ds(64 * (p % 2), 64), pl.ds(128 * (p // 2), 128)])

    rs_a(0)
    rs_b(0)
    query_rows(3)
    send(qback_out, qback, h_s.at[1], h_r.at[1], ((c + 1) % 16, e))
    rs_c(0)
    rs_b(1)
    rs_d(0)
    rs_c(1)
    rs_a(1)
    rs_d(1)
    rs_b(2)
    rs_c(2)
    rs_b(3)
    store(qgrad_ref.at[pl.ds(SPAN, 3 * SPAN)], qgrad_hbm.at[pl.ds(SPAN, 3 * SPAN)])
    rs_d(2)
    rs_c(3)
    rs_d(3)

    landed(qback, h_r.at[1])
    live = jnp.where(c == 0, 0.0, 1.0)
    last_row = lax.broadcasted_iota(jnp.int32, (SPAN, DH), 0) == SPAN - 1
    for h in range(8):
        cols = slice(h * DH, (h + 1) * DH)
        head = qback[:, cols].astype(F32) * live
        qgrad_ref[0:SPAN, cols] = jnp.where(last_row, dqwin[0:1, cols], head).astype(BF16)
    store(qgrad_ref.at[pl.ds(0, SPAN)], qgrad_hbm.at[pl.ds(0, SPAN)])

    for p in range(4):
        rs_e(p)
    for cp in outs:
        cp.wait()
    sent(halo, h_s.at[0])
    sent(qback, h_s.at[1])
    for step, ref in enumerate((line.at[0], line.at[0, pl.ds(0, 2)], gt_out, gm_out)):
        sent(ref, g_s.at[step])
    for step, ref in enumerate((kw_all.at[0], kw_all.at[0, pl.ds(0, 2)], kw_all, kw_all.at[pl.ds(0, 2)])):
        sent(ref, w_s.at[step])
    for step, ref in enumerate((ebuf.at[0, pl.ds(0, 4)], ebuf.at[0, pl.ds(0, 2)], ebuf.at[0])):
        sent(ref, e_s.at[step])
    for step, ref in enumerate((sib_out, t_out, m_out)):
        sent(ref, rs_s.at[step])
    sent(ret_out.at[:, pl.ds(0, 15)], ret_s.at[0])


def shards(queries, out_grad, nbr_states, key_weight, value_weight, q_gain, k_gain, nbr_owner, nbr_slot):
    cos, sin = rope_tables()
    hbm = pl.BlockSpec(memory_space=pl.ANY)
    dma = pltpu.SemaphoreType.DMA
    vmem = pltpu.VMEM
    return pl.pallas_call(
        kernel,
        out_shape=(
            jax.ShapeDtypeStruct((256, 1024), BF16),
            jax.ShapeDtypeStruct((4, NT, 256), F32),
        ),
        in_specs=[hbm] * 11,
        out_specs=(hbm, hbm),
        scratch_shapes=[
            vmem((256, 1024), BF16),
            vmem((256, 1024), BF16),
            vmem((1, 1024), F32),
            vmem((1, 1024), F32),
            vmem((256, DH), F32),
            vmem((256, DH), F32),
            vmem((256, 1024), BF16),
            vmem((4, 4, 64, 128), F32),
            vmem((2, 4, 4, NT, 128), BF16),
            vmem((2, 2, 4, NT, 128), BF16),
            vmem((2, 2, 4, NT, 128), BF16),
            vmem((2, 2, 8, NT, 128), BF16),
            vmem((2, 2, 8, NT, 128), BF16),
            vmem((CHUNKS, 4, 4, 128, CW), BF16),
            vmem((CHUNKS, 4, 4, 128, CW), BF16),
            vmem((2, 8, 1024, 128), BF16),
            vmem((2, SPAN, 1024), BF16),
            vmem((8, 4 * SPAN, DH), F32),
            vmem((4, 4, 2 * SPAN, 256), BF16),
            vmem((4, 4, 2 * SPAN, 256), BF16),
            vmem((4 * SPAN, 1024), F32),
            vmem((SPAN, 1024), BF16),
            vmem((SPAN, 1024), BF16),
            vmem((1024, 2 * CW), BF16),
            vmem((2, 256, CW), F32),
            vmem((2, 256, CW), BF16),
            vmem((2, 2, 4, 1024, 128), F32),
            vmem((2, 4, 1024, 128), BF16),
            vmem((2, 4, 1024, 128), BF16),
            vmem((4, 2, 256, 128), BF16),
            vmem((4, 2, 256, 128), BF16),
            vmem((4, 2, 2, 256, 128), BF16),
            vmem((4, 2, 2, 256, 128), BF16),
            vmem((4, 8, 64, 128), F32),
            vmem((4, 16, 2, 64, 128), BF16),
            vmem((4, 16, 2, 64, 128), BF16),
            pltpu.SMEM((5, 16), jnp.int32),
            pltpu.SMEM((2, 64), jnp.int32),
            pltpu.SMEM((2, 64), jnp.int32),
            dma((18,)),
            dma((6,)),
            dma((4,)),
            dma((CHUNKS, 4)),
            dma((4,)),
            dma((4,)),
            dma((3,)),
            dma((2, 3)),
            dma((2,)),
            dma((2,)),
            dma((3,)),
            dma((4, 3)),
            dma((1,)),
            dma((4,)),
        ],
        compiler_params=pltpu.CompilerParams(
            collective_id=0, has_side_effects=True, vmem_limit_bytes=60 * 2**20
        ),
    )(
        queries, out_grad, nbr_states, key_weight, value_weight,
        q_gain.reshape(1, -1), k_gain.reshape(1, -1), jnp.asarray(cos), jnp.asarray(sin),
        nbr_owner.T, nbr_slot.T,
    )


def solution(mesh):
    in_specs = (
        P("ctx", "enc"),
        P("ctx", "enc"),
        P("ctx", None, "enc"),
        P("ctx", "enc"),
        P("ctx", "enc"),
        P("enc"),
        P("enc"),
        P(),
        P(),
    )
    out_specs = (P("ctx", "enc"), P("ctx", None, "enc"))
    return jax.shard_map(shards, mesh=mesh, in_specs=in_specs, out_specs=out_specs, check_vma=False)
```

```python
import functools

import jax
import jax.numpy as jnp
import numpy as np
from jax import lax
from jax.experimental import pallas as pl
from jax.experimental.pallas import tpu as pltpu
from jax.sharding import PartitionSpec as P

MESH = pl.DeviceIdType.MESH
F32 = jnp.float32
BF16 = jnp.bfloat16

DH = 128
SPAN = 64
NT = 128
EPSILON = 1e-06
LOG_BASE = 9.210340371976184
SCALE = DH**-0.5
CHUNKS = 4
CW = 256

NT_DIMS = (((1,), (1,)), ((), ()))
TN_DIMS = (((0,), (0,)), ((), ()))


def rope_tables():
    half = DH // 2
    freq = np.exp(np.arange(half) * (-2.0 * LOG_BASE / DH))
    angle = np.arange(NT)[:, None] * freq[None, :]
    cos = np.concatenate([np.cos(angle)] * 2, axis=1)
    sin = np.concatenate([-np.sin(angle), np.sin(angle)], axis=1)
    twice = lambda t: np.concatenate([t, t], axis=0).astype(np.float32)
    return twice(cos), twice(sin)


def swap(v):
    return pltpu.roll(v, DH // 2, 1)


def unit(v):
    r = lax.rsqrt(jnp.mean(v * v, axis=1, keepdims=True) + EPSILON)
    return v * r, r


def rope(v, cos, sin):
    return v * cos + swap(v) * sin


def rope_back(d, cos, sin):
    return d * cos + swap(d * sin)


def unit_back(d, xhat, r):
    return r * (d - xhat * jnp.mean(d * xhat, axis=1, keepdims=True))


def kernel(
    q_hbm, do_hbm, pool_hbm, kw_hbm, vw_hbm, qg_hbm, kg_hbm, cos_hbm, sin_hbm, owner_hbm, slot_hbm,
    qgrad_hbm, sgrad_hbm,
    q_ref, do_ref, qg_ref, kg_ref, cos_ref, sin_ref, qgrad_ref, sgrad_ref,
    line, gt_out, gt_in, gm_out, gm_in, kw_all, vw_all, ebuf, halo, qwin, qbd, dobd, dqwin, qback_out, qback, dkv, kps, vps,
    acc, sib_out, sib_in, t_out, t_in, m_out, m_in, refg, ret_out, ret_in, stab, owner_ref, slot_ref,
    in_s, out_s, w_s, w_r, g_s, g_r, e_s, e_r, h_s, h_r, rs_s, rs_r, ret_s, ret_r,
):
    c, e = lax.axis_index("ctx"), lax.axis_index("enc")
    z, x = c // 4, c % 4
    y, core = e // 2, e % 2
    up, dn, opp = (y + 1) % 4, (y + 3) % 4, (y + 2) % 4
    enc = lambda y_, core_: y_ * 2 + core_
    other = (c, enc(y, 1 - core))

    def descriptor(src, dst, ssem, rsem, dev):
        return pltpu.make_async_remote_copy(
            src_ref=src, dst_ref=dst, send_sem=ssem, recv_sem=rsem, device_id=dev, device_id_type=MESH
        )

    def send(src, dst, ssem, rsem, dev):
        descriptor(src, dst, ssem, rsem, dev).start()

    def landed(ref, sem):
        descriptor(ref, ref, sem, sem, other).wait_recv()

    def sent(ref, sem):
        descriptor(ref, ref, sem, sem, other).wait_send()

    def load(src, dst, i):
        cp = pltpu.make_async_copy(src, dst, in_s.at[i])
        cp.start()
        return cp

    in_pool = [
        load(pool_hbm.at[:, :, pl.ds(128 * f, 128)], line.at[f, (x, z)[f]], f) for f in range(2)
    ]
    in_small = [load(owner_hbm, owner_ref, 2), load(slot_hbm, slot_ref, 3)]
    in_w = [
        [load(src.at[:, pl.ds(j * CW, CW)], dst.at[j, z, x], 4 + 2 * j + i) for i, (src, dst) in enumerate(((kw_hbm, kw_all), (vw_hbm, vw_all)))]
        for j in range(CHUNKS)
    ]
    in_q = [load(q_hbm, q_ref, 12), load(do_hbm, do_ref, 13)]
    in_small += [
        load(src, dst, 14 + i)
        for i, (src, dst) in enumerate(((qg_hbm, qg_ref), (kg_hbm, kg_ref), (cos_hbm, cos_ref), (sin_hbm, sin_ref)))
    ]

    barrier = pltpu.get_barrier_semaphore()
    for d in range(1, 16):
        pl.semaphore_signal(barrier, inc=1, device_id=((c + d) % 16, e), device_id_type=MESH)
    for there in (enc(up, core), enc(dn, core), enc(y, 1 - core)):
        pl.semaphore_signal(barrier, inc=1, device_id=(c, there), device_id_type=MESH)
    pl.semaphore_wait(barrier, 18)

    class Chunk:
        def __init__(self, j):
            self.j = j

        def view(self, ab, first, second):
            zi, xi = (second, first) if ab == 0 else (first, second)
            return (kw_all, vw_all)[ab].at[self.j, zi, xi]

        def half(self, ab, first, second, h):
            zi, xi = (second, first) if ab == 0 else (first, second)
            return (kw_all, vw_all)[ab].at[self.j, zi, xi, pl.ds(64 * h, 64)]

        def coords(self, ab):
            return (x, z) if ab == 0 else (z, x)

        def dev(self, ab, first, second):
            return (second * 4 + first, e) if ab == 0 else (first * 4 + second, e)

        def go(self, step, ref, to):
            send(ref, ref, w_s.at[step], w_r.at[self.j, step], to)

        def got(self, step):
            block = kw_all.at[self.j]
            landed((block.at[0], block.at[0, pl.ds(0, 2)], block, block.at[pl.ds(0, 2)])[step], w_r.at[self.j, step])

        def s1(self):
            for ab in (0, 1):
                f, s = self.coords(ab)
                for d in (0, 1):
                    self.go(0, self.view(ab, f, s), self.dev(ab, (f + (1, 3)[d]) % 4, s))

        def s2(self):
            self.got(0)
            for ab in (0, 1):
                f, s = self.coords(ab)
                for d in (0, 1):
                    to = self.dev(ab, (f + (1, 3)[d]) % 4, s)
                    self.go(1, self.half(ab, (f + (3, 1)[d]) % 4, s, d), to)

        def s3(self):
            self.got(1)
            for ab in (0, 1):
                f, s = self.coords(ab)
                for d in (0, 1):
                    self.go(2, self.view(ab, pl.ds(0, 4), s), self.dev(ab, f, (s + (1, 3)[d]) % 4))

        def s4(self):
            self.got(2)
            for ab in (0, 1):
                f, s = self.coords(ab)
                for d in (0, 1):
                    to = self.dev(ab, f, (s + (1, 3)[d]) % 4)
                    self.go(3, self.view(ab, pl.ds(2 * d, 2), (s + (3, 1)[d]) % 4), to)

        def done(self):
            self.got(3)

    def ahead(f, first, second):
        return (second * 4 + first, e) if f == 0 else (first * 4 + second, e)

    def referred(f, second, r):
        to = ahead(f, (x, z)[f], second)[0]
        o, n = owner_ref[r % 2, to * 4 + r // 2], slot_ref[r % 2, to * 4 + r // 2]
        first, there = (o % 4, o // 4) if f == 0 else (o // 4, o % 4)
        block = line[f, first, n]
        return jnp.where(there == (z, x)[f], block, jnp.zeros_like(block))

    def pool1():
        for f in range(2):
            a, b = ((x, z), (z, x))[f]
            for d in (0, 1):
                ref = line.at[f, a]
                send(ref, ref, g_s.at[0], g_r.at[0], ahead(f, (a + (1, 3)[d]) % 4, b))

    def pool2():
        landed(line.at[0], g_r.at[0])
        for f in range(2):
            a, b = ((x, z), (z, x))[f]
            for d in (0, 1):
                ref = line.at[f, (a + (3, 1)[d]) % 4, pl.ds(2 * d, 2)]
                send(ref, ref, g_s.at[1], g_r.at[1], ahead(f, (a + (1, 3)[d]) % 4, b))

    def pool3():
        landed(line.at[0, pl.ds(0, 2)], g_r.at[1])
        for f in range(2):
            a, b = ((x, z), (z, x))[f]
            for d in (0, 1):
                for r in range(4):
                    gt_out[f, d, r] = referred(f, (b + 2) % 4, 4 * d + r)
                send(gt_out.at[f, d], gt_in.at[f, d], g_s.at[2], g_r.at[2], ahead(f, a, (b + (1, 3)[d]) % 4))
        for f in range(2):
            a, b = ((x, z), (z, x))[f]
            for d in (0, 1):
                to = (b + (1, 3)[d]) % 4
                part = pl.ds(4 * (1 - d), 4)
                for r in range(4):
                    gm_out[f, d, 4 * (1 - d) + r] = referred(f, to, 4 * (1 - d) + r)
                send(gm_out.at[f, d, part], gm_in.at[f, d, part], g_s.at[3], g_r.at[3], ahead(f, a, to))

    def pool4():
        landed(gt_in, g_r.at[2])
        for f in range(2):
            a, b = ((x, z), (z, x))[f]
            for d in (0, 1):
                to = (b + (1, 3)[d]) % 4
                part = pl.ds(4 * d, 4)
                for r in range(4):
                    gm_out[f, d, 4 * d + r] = referred(f, to, 4 * d + r) + gt_in[f, d, r]
                send(gm_out.at[f, d, part], gm_in.at[f, d, part], g_s.at[3], g_r.at[3], ahead(f, a, to))

    w = [Chunk(j) for j in range(CHUNKS)]

    for cp in in_pool:
        cp.wait()
    pool1()
    for cp in in_w[0]:
        cp.wait()
    w[0].s1()
    for cp in in_q:
        cp.wait()
    for i, src in enumerate((q_ref, do_ref)):
        send(src.at[pl.ds(0, SPAN)], halo.at[i], h_s.at[0], h_r.at[0], ((c + 15) % 16, e))
    pool2()
    for pair in in_w[1:]:
        for cp in pair:
            cp.wait()
    for cp in in_small:
        cp.wait()
    w[0].s2()
    w[1].s1()
    pool3()

    def table(p, _):
        first, last, count = jnp.int32(0), jnp.int32(0), jnp.int32(0)
        r_first, r_last, r_count = jnp.int32(0), jnp.int32(0), jnp.int32(0)
        for r in range(8):
            hit = owner_ref[r % 2, c * 4 + r // 2] == p
            first = jnp.where(hit & (count == 0), r, first)
            last = jnp.where(hit, r, last)
            count = count + hit.astype(jnp.int32)
            there = owner_ref[r % 2, p * 4 + r // 2] == c
            n = slot_ref[r % 2, p * 4 + r // 2]
            r_first = jnp.where(there & (r_count == 0), n, r_first)
            r_last = jnp.where(there, n, r_last)
            r_count = r_count + there.astype(jnp.int32)
        stab[0, p], stab[1, p], stab[2, p] = first, last, count
        stab[3, p] = jnp.where(r_count > 0, r_first, -1)
        stab[4, p] = jnp.where(r_count > 1, r_last, -1)
        return 0

    lax.fori_loop(0, 16, table, 0)

    landed(halo, h_r.at[0])
    keep = jnp.where(c == 15, 0.0, 1.0)
    first_row = lax.broadcasted_iota(jnp.int32, (4 * SPAN, DH), 0) == 0

    def windows(ref, which, cols):
        own_rows = ref[:, cols].astype(F32)
        nxt = halo[which, :, cols].astype(F32) * keep
        shifted = pltpu.roll(jnp.concatenate([own_rows[SPAN:], nxt], axis=0), 1, 0)
        return jnp.where(first_row, own_rows[SPAN - 1 : SPAN], shifted)

    qcos = jnp.concatenate([cos_ref[0:SPAN, :]] * 4, axis=0)
    qsin = jnp.concatenate([sin_ref[0:SPAN, :]] * 4, axis=0)
    zero = jnp.zeros((SPAN, DH), BF16)

    def prepare(h):
        j, hh = h // 2, h % 2
        cols = pl.ds(h * DH, DH)
        v = windows(q_ref, 0, cols)
        qwin[h] = v
        xhat, _ = unit(v)
        rot = (rope(xhat * qg_ref[:, cols], qcos, qsin) * SCALE).astype(BF16)
        dov = windows(do_ref, 1, cols).astype(BF16)
        for s in range(4):
            r = slice(s * SPAN, (s + 1) * SPAN)
            mine = slice(hh * DH, (hh + 1) * DH)
            rest = slice((1 - hh) * DH, (2 - hh) * DH)
            rows = slice(hh * SPAN, (hh + 1) * SPAN)
            qbd[j, s, rows, mine] = rot[r]
            qbd[j, s, rows, rest] = zero
            dobd[j, s, rows, mine] = dov[r]
            dobd[j, s, rows, rest] = zero

    for h in range(4):
        prepare(h)
    pool4()
    w[0].s3()
    for h in range(4, 8):
        prepare(h)


    def to_sibling(f, slot):
        ref = ebuf.at[f, slot]
        send(ref, ref, e_s.at[2], e_r.at[f, 2], other)

    def y1(f):
        b = (z, x)[f]
        for r in range(8):
            ebuf[f, e, r * NT : (r + 1) * NT, :] = referred(f, b, r) + gm_in[f, 0, r] + gm_in[f, 1, r]
        for to in (up, dn):
            ref = ebuf.at[f, e]
            send(ref, ref, e_s.at[0], e_r.at[f, 0], (c, enc(to, core)))
        to_sibling(f, e)

    def y2(f):
        landed(ebuf.at[f, pl.ds(0, 2)], e_r.at[f, 0])
        for d, frm, to in ((0, dn, up), (1, up, dn)):
            slot = enc(frm, core)
            part = ebuf.at[f, slot, pl.ds(512 * d, 512)]
            send(part, part, e_s.at[1], e_r.at[f, 1], (c, enc(to, core)))
            to_sibling(f, slot)

    def y3(f):
        landed(ebuf.at[f, 0], e_r.at[f, 1])
        to_sibling(f, enc(opp, core))

    landed(gm_in, g_r.at[3])
    y1(0)
    y1(1)
    w[1].s2()
    w[3].s1()
    w[2].s1()
    w[1].s3()
    w[2].s2()
    w[3].s2()
    y2(0)
    w[0].s4()
    y2(1)
    w[2].s3()
    y3(0)
    y3(1)
    w[1].s4()
    w[0].done()
    for f in range(2):
        landed(ebuf.at[f, pl.ds(0, 4)], e_r.at[f, 2])

    def project(j, s):
        rows = slice(s * 256, (s + 1) * 256)
        ecat = jnp.concatenate([ebuf[f, i, rows, :] for i in range(8) for f in range(2)], axis=1)
        kw, vw = kw_all[j].reshape(2048, CW), vw_all[j].reshape(2048, CW)
        kps[s % 2] = jnp.dot(ecat, kw, preferred_element_type=F32).astype(BF16).astype(F32)
        vps[s % 2] = jnp.dot(ecat, vw, preferred_element_type=F32).astype(BF16)

    def keep_rows(s, cols, v):
        for rr in range(2):
            for h in range(2):
                to = h * 512 + (2 * s + rr) * 64
                dkv[to : to + 64, cols] = v[rr * NT + h * 64 : rr * NT + h * 64 + 64]

    def attend(j, s):
        rows = slice(s * 256, (s + 1) * 256)
        kp, vp = kps[s % 2], vps[s % 2]
        cos, sin = cos_ref[...], sin_ref[...]
        hats, rs, gains, ks = [], [], [], []
        for hh in range(2):
            xhat, r = unit(kp[:, hh * DH : (hh + 1) * DH])
            g = kg_ref[:, (2 * j + hh) * DH : (2 * j + hh + 1) * DH]
            ks.append(rope(xhat * g, cos, sin).astype(BF16))
            hats.append(xhat)
            rs.append(r)
            gains.append(g)
        k = jnp.concatenate(ks, axis=1)
        qb, dob = qbd[j, s], dobd[j, s]
        scores = lax.dot_general(k, qb, NT_DIMS, preferred_element_type=F32)
        dp = lax.dot_general(vp, dob, NT_DIMS, preferred_element_type=F32)
        p = jnp.exp(scores)
        p = p * (1.0 / jnp.sum(p, axis=0, keepdims=True))
        ds = (p * (dp - jnp.sum(p * dp, axis=0, keepdims=True))).astype(BF16)
        dv = jnp.dot(p.astype(BF16), dob, preferred_element_type=F32)
        dk = jnp.dot(ds, qb, preferred_element_type=F32)
        dq = lax.dot_general(ds, k, TN_DIMS, preferred_element_type=F32) * SCALE
        for hh in range(2):
            cols = slice(hh * DH, (hh + 1) * DH)
            d = rope_back(dk[:, cols], cos, sin) * gains[hh]
            keep_rows(s, cols, unit_back(d, hats[hh], rs[hh]).astype(BF16))
        keep_rows(s, slice(CW, 2 * CW), dv.astype(BF16))
        qrows = slice(s * SPAN, (s + 1) * SPAN)
        for hh in range(2):
            h = 2 * j + hh
            xhat, r = unit(qwin[h, qrows, :])
            d = dq[hh * SPAN : (hh + 1) * SPAN, hh * DH : (hh + 1) * DH]
            d = rope_back(d, cos_ref[0:SPAN, :], sin_ref[0:SPAN, :]) * qg_ref[:, h * DH : (h + 1) * DH]
            dqwin[qrows, h * DH : (h + 1) * DH] = unit_back(d, xhat, r)

    def compute(j, part):
        if part == 0:
            project(j, 0)
        for s in (2 * part, 2 * part + 1):
            if s < 3:
                project(j, s + 1)
            attend(j, s)

    def product(j, f, which):
        xi = 2 * (core if which else 1 - core) + f
        for i in range(2):
            wcat = jnp.concatenate([b[j, 2 * i : 2 * i + 2, xi].reshape(256, CW) for b in (kw_all, vw_all)], axis=1)
            part = lax.dot_general(dkv[...], wcat, NT_DIMS, preferred_element_type=F32)
            for k in range(2):
                new = part[:, k * 128 : (k + 1) * 128]
                if j > 0:
                    new = new + acc[f, which, 2 * i + k]
                if j == CHUNKS - 1 and which == 0:
                    sib_out[f, 2 * i + k] = new.astype(BF16)
                else:
                    acc[f, which, 2 * i + k] = new

    def products(j):
        for f in range(2):
            for which in range(2):
                product(j, f, which)

    def query_rows(j):
        for h in (2 * j, 2 * j + 1):
            cols = slice(h * DH, (h + 1) * DH)
            back = pltpu.roll(dqwin[:, cols], 4 * SPAN - 1, 0).astype(BF16)
            qgrad_ref[SPAN:, cols] = back[: 3 * SPAN]
            qback_out[:, cols] = back[3 * SPAN :]

    compute(0, 0)
    compute(0, 1)
    w[2].s4()
    products(0)
    w[3].s3()
    w[1].done()
    compute(1, 0)
    compute(1, 1)
    products(1)
    query_rows(0)
    query_rows(1)
    w[2].done()
    compute(2, 0)
    w[3].s4()
    compute(2, 1)
    products(2)
    query_rows(2)
    w[3].done()
    compute(3, 0)
    compute(3, 1)

    def rs_send(p, k, src, dst, to):
        send(src, dst, rs_s.at[k], rs_r.at[p, k], to)

    def rs_a(f):
        product(CHUNKS - 1, f, 0)
        for h in range(2):
            rows = pl.ds(512 * h, 512)
            rs_send(2 * f + h, 0, sib_out.at[f, :, rows], sib_in.at[f, :, rows], other)
        product(CHUNKS - 1, f, 1)

    def both(p, i, start, size):
        rows = pl.ds(512 * (p % 2) + start, size)
        return acc[p // 2, 1, i, rows, :] + sib_in[p // 2, i, rows, :].astype(F32)

    sides = ((0, up), (1, dn))

    def rs_b(p):
        landed(sib_in.at[p // 2, :, pl.ds(512 * (p % 2), 512)], rs_r.at[p, 0])
        for d, to in sides:
            t_out[p, d] = both(p, opp, 256 * d, 256).astype(BF16)
            rs_send(p, 1, t_out.at[p, d], t_in.at[p, d], (c, enc(to, core)))
        for d, to in sides:
            m_out[p, d, 1 - d] = both(p, to, 256 * (1 - d), 256).astype(BF16)
            rs_send(p, 2, m_out.at[p, d, 1 - d], m_in.at[p, d, 1 - d], (c, enc(to, core)))

    def rs_c(p):
        landed(t_in.at[p], rs_r.at[p, 1])
        for d, to in sides:
            m_out[p, d, d] = (both(p, to, 256 * d, 256) + t_in[p, d].astype(F32)).astype(BF16)
            rs_send(p, 2, m_out.at[p, d, d], m_in.at[p, d, d], (c, enc(to, core)))

    def rs_d(p):
        landed(m_in.at[p], rs_r.at[p, 2])
        for h in range(2):
            total = both(p, y, 256 * h, 256) + m_in[p, 0, h].astype(F32) + m_in[p, 1, h].astype(F32)
            refg[p, 4 * h : 4 * h + 4] = total.astype(BF16).reshape(4, 64, 128)
        for d in range(16):
            to = (c + d) % 16
            count = stab[2, to]
            none = jnp.zeros((64, 128), BF16)
            block0 = jnp.where(count > 0, refg[p, stab[0, to]], none)
            block1 = jnp.where(count > 1, refg[p, stab[1, to]], none)
            if d == 0:
                ret_in[p, c, 0] = block0
                ret_in[p, c, 1] = block1
                continue
            ret_out[p, d, 0] = block0
            ret_out[p, d, 1] = block1
            send(ret_out.at[p, d], ret_in.at[p, c], ret_s.at[0], ret_r.at[p], (to, e))

    outs = []

    def store(src, dst):
        cp = pltpu.make_async_copy(src, dst, out_s.at[len(outs)])
        cp.start()
        outs.append(cp)

    def rs_e(p):
        landed(ret_in.at[p, pl.ds(0, 15)], ret_r.at[p])

        def add(o, sums):
            b0, b1 = ret_in[p, o, 0].astype(F32), ret_in[p, o, 1].astype(F32)
            n0, n1 = stab[3, o], stab[4, o]
            return tuple(
                a + b0 * jnp.where(n0 == n, 1.0, 0.0) + b1 * jnp.where(n1 == n, 1.0, 0.0)
                for n, a in enumerate(sums)
            )

        for n, a in enumerate(lax.fori_loop(0, 16, add, tuple(jnp.zeros((64, 128), F32) for _ in range(4)))):
            sgrad_ref[p, n] = a
        store(sgrad_ref.at[p], sgrad_hbm.at[:, pl.ds(64 * (p % 2), 64), pl.ds(128 * (p // 2), 128)])

    rs_a(0)
    rs_b(0)
    query_rows(3)
    send(qback_out, qback, h_s.at[1], h_r.at[1], ((c + 1) % 16, e))
    rs_a(1)
    rs_c(0)
    rs_b(1)
    rs_d(0)
    rs_c(1)
    rs_b(2)
    rs_d(1)
    rs_c(2)
    rs_b(3)
    rs_d(2)
    rs_c(3)
    store(qgrad_ref.at[pl.ds(SPAN, 3 * SPAN)], qgrad_hbm.at[pl.ds(SPAN, 3 * SPAN)])
    rs_d(3)

    landed(qback, h_r.at[1])
    live = jnp.where(c == 0, 0.0, 1.0)
    last_row = lax.broadcasted_iota(jnp.int32, (SPAN, DH), 0) == SPAN - 1
    for h in range(8):
        cols = slice(h * DH, (h + 1) * DH)
        head = qback[:, cols].astype(F32) * live
        qgrad_ref[0:SPAN, cols] = jnp.where(last_row, dqwin[0:1, cols], head).astype(BF16)
    store(qgrad_ref.at[pl.ds(0, SPAN)], qgrad_hbm.at[pl.ds(0, SPAN)])

    for p in range(4):
        rs_e(p)
    for cp in outs:
        cp.wait()
    sent(halo, h_s.at[0])
    sent(qback, h_s.at[1])
    for step, ref in enumerate((line.at[0], line.at[0, pl.ds(0, 2)], gt_out, gm_out)):
        sent(ref, g_s.at[step])
    for step, ref in enumerate((kw_all.at[0], kw_all.at[0, pl.ds(0, 2)], kw_all, kw_all.at[pl.ds(0, 2)])):
        sent(ref, w_s.at[step])
    for step, ref in enumerate((ebuf.at[0, pl.ds(0, 4)], ebuf.at[0, pl.ds(0, 2)], ebuf.at[0])):
        sent(ref, e_s.at[step])
    for step, ref in enumerate((sib_out, t_out, m_out)):
        sent(ref, rs_s.at[step])
    sent(ret_out.at[:, pl.ds(0, 15)], ret_s.at[0])


def shards(queries, out_grad, nbr_states, key_weight, value_weight, q_gain, k_gain, nbr_owner, nbr_slot):
    cos, sin = rope_tables()
    hbm = pl.BlockSpec(memory_space=pl.ANY)
    dma = pltpu.SemaphoreType.DMA
    vmem = pltpu.VMEM
    return pl.pallas_call(
        kernel,
        out_shape=(
            jax.ShapeDtypeStruct((256, 1024), BF16),
            jax.ShapeDtypeStruct((4, NT, 256), F32),
        ),
        in_specs=[hbm] * 11,
        out_specs=(hbm, hbm),
        scratch_shapes=[
            vmem((256, 1024), BF16),
            vmem((256, 1024), BF16),
            vmem((1, 1024), F32),
            vmem((1, 1024), F32),
            vmem((256, DH), F32),
            vmem((256, DH), F32),
            vmem((256, 1024), BF16),
            vmem((4, 4, 64, 128), F32),
            vmem((2, 4, 4, NT, 128), BF16),
            vmem((2, 2, 4, NT, 128), BF16),
            vmem((2, 2, 4, NT, 128), BF16),
            vmem((2, 2, 8, NT, 128), BF16),
            vmem((2, 2, 8, NT, 128), BF16),
            vmem((CHUNKS, 4, 4, 128, CW), BF16),
            vmem((CHUNKS, 4, 4, 128, CW), BF16),
            vmem((2, 8, 1024, 128), BF16),
            vmem((2, SPAN, 1024), BF16),
            vmem((8, 4 * SPAN, DH), F32),
            vmem((4, 4, 2 * SPAN, 256), BF16),
            vmem((4, 4, 2 * SPAN, 256), BF16),
            vmem((4 * SPAN, 1024), F32),
            vmem((SPAN, 1024), BF16),
            vmem((SPAN, 1024), BF16),
            vmem((1024, 2 * CW), BF16),
            vmem((2, 256, CW), F32),
            vmem((2, 256, CW), BF16),
            vmem((2, 2, 4, 1024, 128), F32),
            vmem((2, 4, 1024, 128), BF16),
            vmem((2, 4, 1024, 128), BF16),
            vmem((4, 2, 256, 128), BF16),
            vmem((4, 2, 256, 128), BF16),
            vmem((4, 2, 2, 256, 128), BF16),
            vmem((4, 2, 2, 256, 128), BF16),
            vmem((4, 8, 64, 128), BF16),
            vmem((4, 16, 2, 64, 128), BF16),
            vmem((4, 16, 2, 64, 128), BF16),
            pltpu.SMEM((5, 16), jnp.int32),
            pltpu.SMEM((2, 64), jnp.int32),
            pltpu.SMEM((2, 64), jnp.int32),
            dma((18,)),
            dma((6,)),
            dma((4,)),
            dma((CHUNKS, 4)),
            dma((4,)),
            dma((4,)),
            dma((3,)),
            dma((2, 3)),
            dma((2,)),
            dma((2,)),
            dma((3,)),
            dma((4, 3)),
            dma((1,)),
            dma((4,)),
        ],
        compiler_params=pltpu.CompilerParams(
            collective_id=0, has_side_effects=True, vmem_limit_bytes=60 * 2**20
        ),
    )(
        queries, out_grad, nbr_states, key_weight, value_weight,
        q_gain.reshape(1, -1), k_gain.reshape(1, -1), jnp.asarray(cos), jnp.asarray(sin),
        nbr_owner.T, nbr_slot.T,
    )


def solution(mesh):
    in_specs = (
        P("ctx", "enc"),
        P("ctx", "enc"),
        P("ctx", None, "enc"),
        P("ctx", "enc"),
        P("ctx", "enc"),
        P("enc"),
        P("enc"),
        P(),
        P(),
    )
    out_specs = (P("ctx", "enc"), P("ctx", None, "enc"))
    return jax.shard_map(shards, mesh=mesh, in_specs=in_specs, out_specs=out_specs, check_vma=False)
```

```python
import functools

import jax
import jax.numpy as jnp
import numpy as np
from jax import lax
from jax.experimental import pallas as pl
from jax.experimental.pallas import tpu as pltpu
from jax.sharding import PartitionSpec as P

MESH = pl.DeviceIdType.MESH
F32 = jnp.float32
BF16 = jnp.bfloat16

DH = 128
SPAN = 64
NT = 128
EPSILON = 1e-06
LOG_BASE = 9.210340371976184
SCALE = DH**-0.5
CHUNKS = 4
CW = 256

NT_DIMS = (((1,), (1,)), ((), ()))
TN_DIMS = (((0,), (0,)), ((), ()))


def rope_tables():
    half = DH // 2
    freq = np.exp(np.arange(half) * (-2.0 * LOG_BASE / DH))
    angle = np.arange(NT)[:, None] * freq[None, :]
    cos = np.concatenate([np.cos(angle)] * 2, axis=1)
    sin = np.concatenate([-np.sin(angle), np.sin(angle)], axis=1)
    twice = lambda t: np.concatenate([t, t], axis=0).astype(np.float32)
    return twice(cos), twice(sin)


def swap(v):
    return pltpu.roll(v, DH // 2, 1)


def unit(v):
    r = lax.rsqrt(jnp.mean(v * v, axis=1, keepdims=True) + EPSILON)
    return v * r, r


def rope(v, cos, sin):
    return v * cos + swap(v) * sin


def rope_back(d, cos, sin):
    return d * cos + swap(d * sin)


def unit_back(d, xhat, r):
    return r * (d - xhat * jnp.mean(d * xhat, axis=1, keepdims=True))


def kernel(
    q_hbm, do_hbm, pool_hbm, kw_hbm, vw_hbm, qg_hbm, kg_hbm, cos_hbm, sin_hbm, owner_hbm, slot_hbm,
    qgrad_ref, sgrad_ref,
    q_ref, do_ref, qg_ref, kg_ref, cos_ref, sin_ref,
    line, gt_out, gt_in, gm_out, gm_in, kw_all, vw_all, ebuf, halo, qwin, qbd, dobd, dqwin, qback_out, qback, dkv, kps, vps, early,
    acc, sib_out, sib_in, t_out, t_in, m_out, m_in, refg, ret_out, ret_in, stab, owner_ref, slot_ref,
    in_s, w_s, w_r, g_s, g_r, e_s, e_r, h_s, h_r, rs_s, rs_r, ret_s, ret_r,
):
    c, e = lax.axis_index("ctx"), lax.axis_index("enc")
    z, x = c // 4, c % 4
    y, core = e // 2, e % 2
    up, dn, opp = (y + 1) % 4, (y + 3) % 4, (y + 2) % 4
    enc = lambda y_, core_: y_ * 2 + core_
    other = (c, enc(y, 1 - core))

    def descriptor(src, dst, ssem, rsem, dev):
        return pltpu.make_async_remote_copy(
            src_ref=src, dst_ref=dst, send_sem=ssem, recv_sem=rsem, device_id=dev, device_id_type=MESH
        )

    def send(src, dst, ssem, rsem, dev):
        descriptor(src, dst, ssem, rsem, dev).start()

    def landed(ref, sem):
        descriptor(ref, ref, sem, sem, other).wait_recv()

    def sent(ref, sem):
        descriptor(ref, ref, sem, sem, other).wait_send()

    def load(src, dst, i):
        cp = pltpu.make_async_copy(src, dst, in_s.at[i])
        cp.start()
        return cp

    in_pool = [
        load(pool_hbm.at[:, :, pl.ds(128 * f, 128)], line.at[f, (x, z)[f]], f) for f in range(2)
    ]
    in_small = [load(owner_hbm, owner_ref, 2), load(slot_hbm, slot_ref, 3)]
    in_w = [
        [load(src.at[:, pl.ds(j * CW, CW)], dst.at[j, z, x], 4 + 2 * j + i) for i, (src, dst) in enumerate(((kw_hbm, kw_all), (vw_hbm, vw_all)))]
        for j in range(CHUNKS)
    ]
    in_q = [load(q_hbm, q_ref, 12), load(do_hbm, do_ref, 13)]
    in_small += [
        load(src, dst, 14 + i)
        for i, (src, dst) in enumerate(((qg_hbm, qg_ref), (kg_hbm, kg_ref), (cos_hbm, cos_ref), (sin_hbm, sin_ref)))
    ]

    barrier = pltpu.get_barrier_semaphore()
    for d in range(1, 16):
        pl.semaphore_signal(barrier, inc=1, device_id=((c + d) % 16, e), device_id_type=MESH)
    for there in (enc(up, core), enc(dn, core), enc(y, 1 - core)):
        pl.semaphore_signal(barrier, inc=1, device_id=(c, there), device_id_type=MESH)
    pl.semaphore_wait(barrier, 18)

    class Chunk:
        def __init__(self, j):
            self.j = j

        def view(self, ab, first, second):
            zi, xi = (second, first) if ab == 0 else (first, second)
            return (kw_all, vw_all)[ab].at[self.j, zi, xi]

        def half(self, ab, first, second, h):
            zi, xi = (second, first) if ab == 0 else (first, second)
            return (kw_all, vw_all)[ab].at[self.j, zi, xi, pl.ds(64 * h, 64)]

        def coords(self, ab):
            return (x, z) if ab == 0 else (z, x)

        def dev(self, ab, first, second):
            return (second * 4 + first, e) if ab == 0 else (first * 4 + second, e)

        def go(self, step, ref, to):
            send(ref, ref, w_s.at[step], w_r.at[self.j, step], to)

        def got(self, step):
            block = kw_all.at[self.j]
            landed((block.at[0], block.at[0, pl.ds(0, 2)], block, block.at[pl.ds(0, 2)])[step], w_r.at[self.j, step])

        def s1(self):
            for ab in (0, 1):
                f, s = self.coords(ab)
                for d in (0, 1):
                    self.go(0, self.view(ab, f, s), self.dev(ab, (f + (1, 3)[d]) % 4, s))

        def s2(self):
            self.got(0)
            for ab in (0, 1):
                f, s = self.coords(ab)
                for d in (0, 1):
                    to = self.dev(ab, (f + (1, 3)[d]) % 4, s)
                    self.go(1, self.half(ab, (f + (3, 1)[d]) % 4, s, d), to)

        def s3(self):
            self.got(1)
            for ab in (0, 1):
                f, s = self.coords(ab)
                for d in (0, 1):
                    self.go(2, self.view(ab, pl.ds(0, 4), s), self.dev(ab, f, (s + (1, 3)[d]) % 4))

        def s4(self):
            self.got(2)
            for ab in (0, 1):
                f, s = self.coords(ab)
                for d in (0, 1):
                    to = self.dev(ab, f, (s + (1, 3)[d]) % 4)
                    self.go(3, self.view(ab, pl.ds(2 * d, 2), (s + (3, 1)[d]) % 4), to)

        def done(self):
            self.got(3)

    def ahead(f, first, second):
        return (second * 4 + first, e) if f == 0 else (first * 4 + second, e)

    def referred(f, second, r):
        to = ahead(f, (x, z)[f], second)[0]
        o, n = owner_ref[r % 2, to * 4 + r // 2], slot_ref[r % 2, to * 4 + r // 2]
        first, there = (o % 4, o // 4) if f == 0 else (o // 4, o % 4)
        block = line[f, first, n]
        return jnp.where(there == (z, x)[f], block, jnp.zeros_like(block))

    def pool1():
        for f in range(2):
            a, b = ((x, z), (z, x))[f]
            for d in (0, 1):
                ref = line.at[f, a]
                send(ref, ref, g_s.at[0], g_r.at[0], ahead(f, (a + (1, 3)[d]) % 4, b))

    def pool2():
        landed(line.at[0], g_r.at[0])
        for f in range(2):
            a, b = ((x, z), (z, x))[f]
            for d in (0, 1):
                ref = line.at[f, (a + (3, 1)[d]) % 4, pl.ds(2 * d, 2)]
                send(ref, ref, g_s.at[1], g_r.at[1], ahead(f, (a + (1, 3)[d]) % 4, b))

    def pool3():
        landed(line.at[0, pl.ds(0, 2)], g_r.at[1])
        for f in range(2):
            a, b = ((x, z), (z, x))[f]
            for d in (0, 1):
                for r in range(4):
                    gt_out[f, d, r] = referred(f, (b + 2) % 4, 4 * d + r)
                send(gt_out.at[f, d], gt_in.at[f, d], g_s.at[2], g_r.at[2], ahead(f, a, (b + (1, 3)[d]) % 4))
        for f in range(2):
            a, b = ((x, z), (z, x))[f]
            for d in (0, 1):
                to = (b + (1, 3)[d]) % 4
                part = pl.ds(4 * (1 - d), 4)
                for r in range(4):
                    gm_out[f, d, 4 * (1 - d) + r] = referred(f, to, 4 * (1 - d) + r)
                send(gm_out.at[f, d, part], gm_in.at[f, d, part], g_s.at[3], g_r.at[3], ahead(f, a, to))

    def pool4():
        landed(gt_in, g_r.at[2])
        for f in range(2):
            a, b = ((x, z), (z, x))[f]
            for d in (0, 1):
                to = (b + (1, 3)[d]) % 4
                part = pl.ds(4 * d, 4)
                for r in range(4):
                    gm_out[f, d, 4 * d + r] = referred(f, to, 4 * d + r) + gt_in[f, d, r]
                send(gm_out.at[f, d, part], gm_in.at[f, d, part], g_s.at[3], g_r.at[3], ahead(f, a, to))

    w = [Chunk(j) for j in range(CHUNKS)]

    for cp in in_pool:
        cp.wait()
    pool1()
    for cp in in_w[0]:
        cp.wait()
    w[0].s1()
    for cp in in_q:
        cp.wait()
    for i, src in enumerate((q_ref, do_ref)):
        send(src.at[pl.ds(0, SPAN)], halo.at[i], h_s.at[0], h_r.at[0], ((c + 15) % 16, e))
    pool2()
    for pair in in_w[1:]:
        for cp in pair:
            cp.wait()
    for cp in in_small:
        cp.wait()
    w[0].s2()
    w[1].s1()
    pool3()

    def table(p, _):
        first, last, count = jnp.int32(0), jnp.int32(0), jnp.int32(0)
        r_first, r_last, r_count = jnp.int32(0), jnp.int32(0), jnp.int32(0)
        for r in range(8):
            hit = owner_ref[r % 2, c * 4 + r // 2] == p
            first = jnp.where(hit & (count == 0), r, first)
            last = jnp.where(hit, r, last)
            count = count + hit.astype(jnp.int32)
            there = owner_ref[r % 2, p * 4 + r // 2] == c
            n = slot_ref[r % 2, p * 4 + r // 2]
            r_first = jnp.where(there & (r_count == 0), n, r_first)
            r_last = jnp.where(there, n, r_last)
            r_count = r_count + there.astype(jnp.int32)
        stab[0, p], stab[1, p], stab[2, p] = first, last, count
        stab[3, p] = jnp.where(r_count > 0, r_first, -1)
        stab[4, p] = jnp.where(r_count > 1, r_last, -1)
        return 0

    lax.fori_loop(0, 16, table, 0)

    landed(halo, h_r.at[0])
    keep = jnp.where(c == 15, 0.0, 1.0)
    first_row = lax.broadcasted_iota(jnp.int32, (4 * SPAN, DH), 0) == 0

    def windows(ref, which, cols):
        own_rows = ref[:, cols].astype(F32)
        nxt = halo[which, :, cols].astype(F32) * keep
        shifted = pltpu.roll(jnp.concatenate([own_rows[SPAN:], nxt], axis=0), 1, 0)
        return jnp.where(first_row, own_rows[SPAN - 1 : SPAN], shifted)

    qcos = jnp.concatenate([cos_ref[0:SPAN, :]] * 4, axis=0)
    qsin = jnp.concatenate([sin_ref[0:SPAN, :]] * 4, axis=0)
    zero = jnp.zeros((SPAN, DH), BF16)

    def prepare(h):
        j, hh = h // 2, h % 2
        cols = pl.ds(h * DH, DH)
        v = windows(q_ref, 0, cols)
        qwin[h] = v
        xhat, _ = unit(v)
        rot = (rope(xhat * qg_ref[:, cols], qcos, qsin) * SCALE).astype(BF16)
        dov = windows(do_ref, 1, cols).astype(BF16)
        for s in range(4):
            r = slice(s * SPAN, (s + 1) * SPAN)
            mine = slice(hh * DH, (hh + 1) * DH)
            rest = slice((1 - hh) * DH, (2 - hh) * DH)
            rows = slice(hh * SPAN, (hh + 1) * SPAN)
            qbd[j, s, rows, mine] = rot[r]
            qbd[j, s, rows, rest] = zero
            dobd[j, s, rows, mine] = dov[r]
            dobd[j, s, rows, rest] = zero

    for h in range(4):
        prepare(h)
    pool4()
    w[0].s3()
    for h in range(4, 8):
        prepare(h)


    def to_sibling(f, slot):
        ref = ebuf.at[f, slot]
        send(ref, ref, e_s.at[2], e_r.at[f, 2], other)

    def y1(f):
        b = (z, x)[f]
        for r in range(8):
            ebuf[f, e, r * NT : (r + 1) * NT, :] = referred(f, b, r) + gm_in[f, 0, r] + gm_in[f, 1, r]
        for to in (up, dn):
            ref = ebuf.at[f, e]
            send(ref, ref, e_s.at[0], e_r.at[f, 0], (c, enc(to, core)))
        to_sibling(f, e)

    def y2(f):
        landed(ebuf.at[f, pl.ds(0, 2)], e_r.at[f, 0])
        for d, frm, to in ((0, dn, up), (1, up, dn)):
            slot = enc(frm, core)
            part = ebuf.at[f, slot, pl.ds(512 * d, 512)]
            send(part, part, e_s.at[1], e_r.at[f, 1], (c, enc(to, core)))
            to_sibling(f, slot)

    def y3(f):
        landed(ebuf.at[f, 0], e_r.at[f, 1])
        to_sibling(f, enc(opp, core))

    landed(gm_in, g_r.at[3])
    y1(0)
    y1(1)
    w[1].s2()
    w[3].s1()
    w[2].s1()
    w[1].s3()
    w[2].s2()
    w[3].s2()
    y2(0)
    w[0].s4()
    y2(1)
    w[2].s3()
    y3(0)
    y3(1)
    w[1].s4()
    w[0].done()
    for f in range(2):
        landed(ebuf.at[f, pl.ds(0, 4)], e_r.at[f, 2])

    def line_part(s, zi, xi):
        rows = slice(s * 256, (s + 1) * 256)
        j = CHUNKS - 1
        e_key = jnp.concatenate([ebuf[i % 2, 2 * zi + i // 2, rows, :] for i in range(4)], axis=1)
        e_value = jnp.concatenate([ebuf[xi % 2, 2 * i + xi // 2, rows, :] for i in range(4)], axis=1)
        return (
            jnp.dot(e_key, kw_all[j, zi].reshape(512, CW), preferred_element_type=F32),
            jnp.dot(e_value, vw_all[j, :, xi].reshape(512, CW), preferred_element_type=F32),
        )

    def project_early():
        for s in range(4):
            parts = [line_part(s, (z + d) % 4, (x + d) % 4) for d in (0, 1, 3)]
            early[0, s] = parts[0][0] + parts[1][0] + parts[2][0]
            early[1, s] = parts[0][1] + parts[1][1] + parts[2][1]

    def project(j, s):
        if j == CHUNKS - 1:
            key, value = line_part(s, (z + 2) % 4, (x + 2) % 4)
            kps[s % 2] = (early[0, s] + key).astype(BF16).astype(F32)
            vps[s % 2] = (early[1, s] + value).astype(BF16)
            return
        rows = slice(s * 256, (s + 1) * 256)
        ecat = jnp.concatenate([ebuf[f, i, rows, :] for i in range(8) for f in range(2)], axis=1)
        kw, vw = kw_all[j].reshape(2048, CW), vw_all[j].reshape(2048, CW)
        kps[s % 2] = jnp.dot(ecat, kw, preferred_element_type=F32).astype(BF16).astype(F32)
        vps[s % 2] = jnp.dot(ecat, vw, preferred_element_type=F32).astype(BF16)

    def keep_rows(s, cols, v):
        for rr in range(2):
            for h in range(2):
                to = h * 512 + (2 * s + rr) * 64
                dkv[to : to + 64, cols] = v[rr * NT + h * 64 : rr * NT + h * 64 + 64]

    def attend(j, s):
        rows = slice(s * 256, (s + 1) * 256)
        kp, vp = kps[s % 2], vps[s % 2]
        cos, sin = cos_ref[...], sin_ref[...]
        hats, rs, gains, ks = [], [], [], []
        for hh in range(2):
            xhat, r = unit(kp[:, hh * DH : (hh + 1) * DH])
            g = kg_ref[:, (2 * j + hh) * DH : (2 * j + hh + 1) * DH]
            ks.append(rope(xhat * g, cos, sin).astype(BF16))
            hats.append(xhat)
            rs.append(r)
            gains.append(g)
        k = jnp.concatenate(ks, axis=1)
        qb, dob = qbd[j, s], dobd[j, s]
        scores = lax.dot_general(k, qb, NT_DIMS, preferred_element_type=F32)
        dp = lax.dot_general(vp, dob, NT_DIMS, preferred_element_type=F32)
        p = jnp.exp(scores)
        p = p * (1.0 / jnp.sum(p, axis=0, keepdims=True))
        ds = (p * (dp - jnp.sum(p * dp, axis=0, keepdims=True))).astype(BF16)
        dv = jnp.dot(p.astype(BF16), dob, preferred_element_type=F32)
        dk = jnp.dot(ds, qb, preferred_element_type=F32)
        dq = lax.dot_general(ds, k, TN_DIMS, preferred_element_type=F32) * SCALE
        for hh in range(2):
            cols = slice(hh * DH, (hh + 1) * DH)
            d = rope_back(dk[:, cols], cos, sin) * gains[hh]
            keep_rows(s, cols, unit_back(d, hats[hh], rs[hh]).astype(BF16))
        keep_rows(s, slice(CW, 2 * CW), dv.astype(BF16))
        qrows = slice(s * SPAN, (s + 1) * SPAN)
        for hh in range(2):
            h = 2 * j + hh
            xhat, r = unit(qwin[h, qrows, :])
            d = dq[hh * SPAN : (hh + 1) * SPAN, hh * DH : (hh + 1) * DH]
            d = rope_back(d, cos_ref[0:SPAN, :], sin_ref[0:SPAN, :]) * qg_ref[:, h * DH : (h + 1) * DH]
            dqwin[qrows, h * DH : (h + 1) * DH] = unit_back(d, xhat, r)

    def compute(j, part):
        if part == 0:
            project(j, 0)
        for s in (2 * part, 2 * part + 1):
            if s < 3:
                project(j, s + 1)
            attend(j, s)

    def product(j, f, which, start=0, size=1024):
        xi = 2 * (core if which else 1 - core) + f
        for i in range(2):
            wcat = jnp.concatenate([b[j, 2 * i : 2 * i + 2, xi].reshape(256, CW) for b in (kw_all, vw_all)], axis=1)
            rows = slice(start, start + size)
            part = lax.dot_general(dkv[rows, :], wcat, NT_DIMS, preferred_element_type=F32)
            for k in range(2):
                new = part[:, k * 128 : (k + 1) * 128]
                if j > 0:
                    new = new + acc[f, which, 2 * i + k, rows, :]
                if j == CHUNKS - 1 and which == 0:
                    sib_out[f, 2 * i + k, rows, :] = new.astype(BF16)
                else:
                    acc[f, which, 2 * i + k, rows, :] = new

    def products(j):
        for f in range(2):
            for which in range(2):
                product(j, f, which)

    def query_rows(j):
        for h in (2 * j, 2 * j + 1):
            cols = slice(h * DH, (h + 1) * DH)
            back = pltpu.roll(dqwin[:, cols], 4 * SPAN - 1, 0).astype(BF16)
            qgrad_ref[SPAN:, cols] = back[: 3 * SPAN]
            qback_out[:, cols] = back[3 * SPAN :]

    compute(0, 0)
    compute(0, 1)
    w[2].s4()
    products(0)
    w[3].s3()
    w[1].done()
    compute(1, 0)
    compute(1, 1)
    products(1)
    query_rows(0)
    query_rows(1)
    w[2].done()
    compute(2, 0)
    w[3].s4()
    compute(2, 1)
    products(2)
    query_rows(2)
    project_early()
    w[3].done()
    compute(3, 0)
    compute(3, 1)

    def rs_send(p, k, src, dst, to):
        send(src, dst, rs_s.at[k], rs_r.at[p, k], to)

    def rs_a(p):
        f, h = p // 2, p % 2
        product(CHUNKS - 1, f, 0, 512 * h, 512)
        rows = pl.ds(512 * h, 512)
        rs_send(p, 0, sib_out.at[f, :, rows], sib_in.at[f, :, rows], other)
        product(CHUNKS - 1, f, 1, 512 * h, 512)

    def both(p, i, start, size):
        rows = pl.ds(512 * (p % 2) + start, size)
        return acc[p // 2, 1, i, rows, :] + sib_in[p // 2, i, rows, :].astype(F32)

    sides = ((0, up), (1, dn))

    def rs_b(p):
        landed(sib_in.at[p // 2, :, pl.ds(512 * (p % 2), 512)], rs_r.at[p, 0])
        for d, to in sides:
            t_out[p, d] = both(p, opp, 256 * d, 256).astype(BF16)
            rs_send(p, 1, t_out.at[p, d], t_in.at[p, d], (c, enc(to, core)))
        for d, to in sides:
            m_out[p, d, 1 - d] = both(p, to, 256 * (1 - d), 256).astype(BF16)
            rs_send(p, 2, m_out.at[p, d, 1 - d], m_in.at[p, d, 1 - d], (c, enc(to, core)))

    def rs_c(p):
        landed(t_in.at[p], rs_r.at[p, 1])
        for d, to in sides:
            m_out[p, d, d] = (both(p, to, 256 * d, 256) + t_in[p, d].astype(F32)).astype(BF16)
            rs_send(p, 2, m_out.at[p, d, d], m_in.at[p, d, d], (c, enc(to, core)))

    def rs_d(p):
        landed(m_in.at[p], rs_r.at[p, 2])
        for h in range(2):
            total = both(p, y, 256 * h, 256) + m_in[p, 0, h].astype(F32) + m_in[p, 1, h].astype(F32)
            refg[p, 4 * h : 4 * h + 4] = total.astype(BF16).reshape(4, 64, 128)
        for d in range(16):
            to = (c + d) % 16
            count = stab[2, to]
            none = jnp.zeros((64, 128), BF16)
            block0 = jnp.where(count > 0, refg[p, stab[0, to]], none)
            block1 = jnp.where(count > 1, refg[p, stab[1, to]], none)
            if d == 0:
                ret_in[p, c, 0] = block0
                ret_in[p, c, 1] = block1
                continue
            ret_out[p, d, 0] = block0
            ret_out[p, d, 1] = block1
            send(ret_out.at[p, d], ret_in.at[p, c], ret_s.at[0], ret_r.at[p], (to, e))

    def rs_e(p):
        landed(ret_in.at[p, pl.ds(0, 15)], ret_r.at[p])

        def add(o, sums):
            b0, b1 = ret_in[p, o, 0].astype(F32), ret_in[p, o, 1].astype(F32)
            n0, n1 = stab[3, o], stab[4, o]
            return tuple(
                a + b0 * jnp.where(n0 == n, 1.0, 0.0) + b1 * jnp.where(n1 == n, 1.0, 0.0)
                for n, a in enumerate(sums)
            )

        for n, a in enumerate(lax.fori_loop(0, 16, add, tuple(jnp.zeros((64, 128), F32) for _ in range(4)))):
            sgrad_ref[n, 64 * (p % 2) : 64 * (p % 2) + 64, 128 * (p // 2) : 128 * (p // 2) + 128] = a

    rs_a(0)
    rs_b(0)
    query_rows(3)
    send(qback_out, qback, h_s.at[1], h_r.at[1], ((c + 1) % 16, e))
    rs_a(1)
    rs_c(0)
    rs_b(1)
    rs_a(2)
    rs_d(0)
    rs_c(1)
    rs_b(2)
    rs_a(3)
    rs_d(1)
    rs_c(2)
    rs_b(3)
    rs_d(2)
    rs_c(3)
    rs_d(3)

    landed(qback, h_r.at[1])
    live = jnp.where(c == 0, 0.0, 1.0)
    last_row = lax.broadcasted_iota(jnp.int32, (SPAN, DH), 0) == SPAN - 1
    for h in range(8):
        cols = slice(h * DH, (h + 1) * DH)
        head = qback[:, cols].astype(F32) * live
        qgrad_ref[0:SPAN, cols] = jnp.where(last_row, dqwin[0:1, cols], head).astype(BF16)

    for p in range(4):
        rs_e(p)
    sent(halo, h_s.at[0])
    sent(qback, h_s.at[1])
    for step, ref in enumerate((line.at[0], line.at[0, pl.ds(0, 2)], gt_out, gm_out)):
        sent(ref, g_s.at[step])
    for step, ref in enumerate((kw_all.at[0], kw_all.at[0, pl.ds(0, 2)], kw_all, kw_all.at[pl.ds(0, 2)])):
        sent(ref, w_s.at[step])
    for step, ref in enumerate((ebuf.at[0, pl.ds(0, 4)], ebuf.at[0, pl.ds(0, 2)], ebuf.at[0])):
        sent(ref, e_s.at[step])
    for step, ref in enumerate((sib_out, t_out, m_out)):
        sent(ref, rs_s.at[step])
    sent(ret_out.at[:, pl.ds(0, 15)], ret_s.at[0])


def shards(queries, out_grad, nbr_states, key_weight, value_weight, q_gain, k_gain, nbr_owner, nbr_slot):
    cos, sin = rope_tables()
    hbm = pl.BlockSpec(memory_space=pl.ANY)
    dma = pltpu.SemaphoreType.DMA
    vmem = pltpu.VMEM
    whole = pl.BlockSpec(memory_space=pltpu.VMEM)
    return pl.pallas_call(
        kernel,
        out_shape=(
            vmem((256, 1024), BF16),
            vmem((4, NT, 256), F32),
        ),
        in_specs=[hbm] * 11,
        out_specs=(whole, whole),
        scratch_shapes=[
            vmem((256, 1024), BF16),
            vmem((256, 1024), BF16),
            vmem((1, 1024), F32),
            vmem((1, 1024), F32),
            vmem((256, DH), F32),
            vmem((256, DH), F32),
            vmem((2, 4, 4, NT, 128), BF16),
            vmem((2, 2, 4, NT, 128), BF16),
            vmem((2, 2, 4, NT, 128), BF16),
            vmem((2, 2, 8, NT, 128), BF16),
            vmem((2, 2, 8, NT, 128), BF16),
            vmem((CHUNKS, 4, 4, 128, CW), BF16),
            vmem((CHUNKS, 4, 4, 128, CW), BF16),
            vmem((2, 8, 1024, 128), BF16),
            vmem((2, SPAN, 1024), BF16),
            vmem((8, 4 * SPAN, DH), F32),
            vmem((4, 4, 2 * SPAN, 256), BF16),
            vmem((4, 4, 2 * SPAN, 256), BF16),
            vmem((4 * SPAN, 1024), F32),
            vmem((SPAN, 1024), BF16),
            vmem((SPAN, 1024), BF16),
            vmem((1024, 2 * CW), BF16),
            vmem((2, 256, CW), F32),
            vmem((2, 256, CW), BF16),
            vmem((2, 4, 256, CW), F32),
            vmem((2, 2, 4, 1024, 128), F32),
            vmem((2, 4, 1024, 128), BF16),
            vmem((2, 4, 1024, 128), BF16),
            vmem((4, 2, 256, 128), BF16),
            vmem((4, 2, 256, 128), BF16),
            vmem((4, 2, 2, 256, 128), BF16),
            vmem((4, 2, 2, 256, 128), BF16),
            vmem((4, 8, 64, 128), BF16),
            vmem((4, 16, 2, 64, 128), BF16),
            vmem((4, 16, 2, 64, 128), BF16),
            pltpu.SMEM((5, 16), jnp.int32),
            pltpu.SMEM((2, 64), jnp.int32),
            pltpu.SMEM((2, 64), jnp.int32),
            dma((18,)),
            dma((4,)),
            dma((CHUNKS, 4)),
            dma((4,)),
            dma((4,)),
            dma((3,)),
            dma((2, 3)),
            dma((2,)),
            dma((2,)),
            dma((3,)),
            dma((4, 3)),
            dma((1,)),
            dma((4,)),
        ],
        compiler_params=pltpu.CompilerParams(
            collective_id=0, has_side_effects=True, vmem_limit_bytes=56 * 2**20
        ),
    )(
        queries, out_grad, nbr_states, key_weight, value_weight,
        q_gain.reshape(1, -1), k_gain.reshape(1, -1), jnp.asarray(cos), jnp.asarray(sin),
        nbr_owner.T, nbr_slot.T,
    )


def solution(mesh):
    in_specs = (
        P("ctx", "enc"),
        P("ctx", "enc"),
        P("ctx", None, "enc"),
        P("ctx", "enc"),
        P("ctx", "enc"),
        P("enc"),
        P("enc"),
        P(),
        P(),
    )
    out_specs = (P("ctx", "enc"), P("ctx", None, "enc"))
    return jax.shard_map(shards, mesh=mesh, in_specs=in_specs, out_specs=out_specs, check_vma=False)
```

```python
import functools

import jax
import jax.numpy as jnp
import numpy as np
from jax import lax
from jax.experimental import pallas as pl
from jax.experimental.pallas import tpu as pltpu
from jax.sharding import PartitionSpec as P

MESH = pl.DeviceIdType.MESH
F32 = jnp.float32
BF16 = jnp.bfloat16

DH = 128
SPAN = 64
NT = 128
EPSILON = 1e-06
LOG_BASE = 9.210340371976184
SCALE = DH**-0.5
CHUNKS = 4
CW = 256

NT_DIMS = (((1,), (1,)), ((), ()))
TN_DIMS = (((0,), (0,)), ((), ()))


def rope_tables():
    half = DH // 2
    freq = np.exp(np.arange(half) * (-2.0 * LOG_BASE / DH))
    angle = np.arange(NT)[:, None] * freq[None, :]
    cos = np.concatenate([np.cos(angle)] * 2, axis=1)
    sin = np.concatenate([-np.sin(angle), np.sin(angle)], axis=1)
    twice = lambda t: np.concatenate([t, t], axis=0).astype(np.float32)
    return twice(cos), twice(sin)


def swap(v):
    return pltpu.roll(v, DH // 2, 1)


def unit(v):
    r = lax.rsqrt(jnp.mean(v * v, axis=1, keepdims=True) + EPSILON)
    return v * r, r


def rope(v, cos, sin):
    return v * cos + swap(v) * sin


def rope_back(d, cos, sin):
    return d * cos + swap(d * sin)


def unit_back(d, xhat, r):
    return r * (d - xhat * jnp.mean(d * xhat, axis=1, keepdims=True))


def kernel(
    q_hbm, do_hbm, pool_hbm, kw_hbm, vw_hbm, qg_hbm, kg_hbm, cos_hbm, sin_hbm, owner_hbm, slot_hbm,
    qgrad_ref, sgrad_ref,
    q_ref, do_ref, qg_ref, kg_ref, cos_ref, sin_ref,
    line, gt_out, gt_in, gm_out, gm_in, kw_all, vw_all, ebuf, halo, qwin, qbd, dobd, dqwin, qback_out, qback, dkv, kps, vps, early,
    acc, sib_out, sib_in, t_out, t_in, m_out, m_in, refg, ret_out, ret_in, stab, owner_ref, slot_ref,
    in_s, w_s, w_r, g_s, g_r, e_s, e_r, h_s, h_r, rs_s, rs_r, ret_s, ret_r,
):
    c, e = lax.axis_index("ctx"), lax.axis_index("enc")
    z, x = c // 4, c % 4
    y, core = e // 2, e % 2
    up, dn, opp = (y + 1) % 4, (y + 3) % 4, (y + 2) % 4
    enc = lambda y_, core_: y_ * 2 + core_
    other = (c, enc(y, 1 - core))

    def descriptor(src, dst, ssem, rsem, dev):
        return pltpu.make_async_remote_copy(
            src_ref=src, dst_ref=dst, send_sem=ssem, recv_sem=rsem, device_id=dev, device_id_type=MESH
        )

    def send(src, dst, ssem, rsem, dev):
        descriptor(src, dst, ssem, rsem, dev).start()

    def landed(ref, sem):
        descriptor(ref, ref, sem, sem, other).wait_recv()

    def sent(ref, sem):
        descriptor(ref, ref, sem, sem, other).wait_send()

    def load(src, dst, i):
        cp = pltpu.make_async_copy(src, dst, in_s.at[i])
        cp.start()
        return cp

    in_pool = [
        load(pool_hbm.at[:, :, pl.ds(128 * f, 128)], line.at[f, (x, z)[f]], f) for f in range(2)
    ]
    in_small = [load(owner_hbm, owner_ref, 2), load(slot_hbm, slot_ref, 3)]
    in_w = [
        [load(src.at[:, pl.ds(j * CW, CW)], dst.at[j, z, x], 4 + 2 * j + i) for i, (src, dst) in enumerate(((kw_hbm, kw_all), (vw_hbm, vw_all)))]
        for j in range(CHUNKS)
    ]
    in_q = [load(q_hbm, q_ref, 12), load(do_hbm, do_ref, 13)]
    in_small += [
        load(src, dst, 14 + i)
        for i, (src, dst) in enumerate(((qg_hbm, qg_ref), (kg_hbm, kg_ref), (cos_hbm, cos_ref), (sin_hbm, sin_ref)))
    ]

    barrier = pltpu.get_barrier_semaphore()
    for d in range(1, 16):
        pl.semaphore_signal(barrier, inc=1, device_id=((c + d) % 16, e), device_id_type=MESH)
    for there in (enc(up, core), enc(dn, core), enc(y, 1 - core)):
        pl.semaphore_signal(barrier, inc=1, device_id=(c, there), device_id_type=MESH)
    pl.semaphore_wait(barrier, 18)

    class Chunk:
        def __init__(self, j):
            self.j = j

        def view(self, ab, first, second):
            zi, xi = (second, first) if ab == 0 else (first, second)
            return (kw_all, vw_all)[ab].at[self.j, zi, xi]

        def half(self, ab, first, second, h):
            zi, xi = (second, first) if ab == 0 else (first, second)
            return (kw_all, vw_all)[ab].at[self.j, zi, xi, pl.ds(64 * h, 64)]

        def coords(self, ab):
            return (x, z) if ab == 0 else (z, x)

        def dev(self, ab, first, second):
            return (second * 4 + first, e) if ab == 0 else (first * 4 + second, e)

        def go(self, step, ref, to):
            send(ref, ref, w_s.at[step], w_r.at[self.j, step], to)

        def got(self, step):
            block = kw_all.at[self.j]
            landed((block.at[0], block.at[0, pl.ds(0, 2)], block, block.at[pl.ds(0, 2)])[step], w_r.at[self.j, step])

        def s1(self):
            for ab in (0, 1):
                f, s = self.coords(ab)
                for d in (0, 1):
                    self.go(0, self.view(ab, f, s), self.dev(ab, (f + (1, 3)[d]) % 4, s))

        def s2(self):
            self.got(0)
            for ab in (0, 1):
                f, s = self.coords(ab)
                for d in (0, 1):
                    to = self.dev(ab, (f + (1, 3)[d]) % 4, s)
                    self.go(1, self.half(ab, (f + (3, 1)[d]) % 4, s, d), to)

        def s3(self):
            self.got(1)
            for ab in (0, 1):
                f, s = self.coords(ab)
                for d in (0, 1):
                    self.go(2, self.view(ab, pl.ds(0, 4), s), self.dev(ab, f, (s + (1, 3)[d]) % 4))

        def s4(self):
            self.got(2)
            for ab in (0, 1):
                f, s = self.coords(ab)
                for d in (0, 1):
                    to = self.dev(ab, f, (s + (1, 3)[d]) % 4)
                    self.go(3, self.view(ab, pl.ds(2 * d, 2), (s + (3, 1)[d]) % 4), to)

        def done(self):
            self.got(3)

    def ahead(f, first, second):
        return (second * 4 + first, e) if f == 0 else (first * 4 + second, e)

    def referred(f, second, r):
        to = ahead(f, (x, z)[f], second)[0]
        o, n = owner_ref[r % 2, to * 4 + r // 2], slot_ref[r % 2, to * 4 + r // 2]
        first, there = (o % 4, o // 4) if f == 0 else (o // 4, o % 4)
        block = line[f, first, n]
        return jnp.where(there == (z, x)[f], block, jnp.zeros_like(block))

    def pool1():
        for f in range(2):
            a, b = ((x, z), (z, x))[f]
            for d in (0, 1):
                ref = line.at[f, a]
                send(ref, ref, g_s.at[0], g_r.at[0], ahead(f, (a + (1, 3)[d]) % 4, b))

    def pool2():
        landed(line.at[0], g_r.at[0])
        for f in range(2):
            a, b = ((x, z), (z, x))[f]
            for d in (0, 1):
                ref = line.at[f, (a + (3, 1)[d]) % 4, pl.ds(2 * d, 2)]
                send(ref, ref, g_s.at[1], g_r.at[1], ahead(f, (a + (1, 3)[d]) % 4, b))

    def pool3():
        landed(line.at[0, pl.ds(0, 2)], g_r.at[1])
        for f in range(2):
            a, b = ((x, z), (z, x))[f]
            for d in (0, 1):
                for r in range(4):
                    gt_out[f, d, r] = referred(f, (b + 2) % 4, 4 * d + r)
                send(gt_out.at[f, d], gt_in.at[f, d], g_s.at[2], g_r.at[2], ahead(f, a, (b + (1, 3)[d]) % 4))
        for f in range(2):
            a, b = ((x, z), (z, x))[f]
            for d in (0, 1):
                to = (b + (1, 3)[d]) % 4
                part = pl.ds(4 * (1 - d), 4)
                for r in range(4):
                    gm_out[f, d, 4 * (1 - d) + r] = referred(f, to, 4 * (1 - d) + r)
                send(gm_out.at[f, d, part], gm_in.at[f, d, part], g_s.at[3], g_r.at[3], ahead(f, a, to))

    def pool4():
        landed(gt_in, g_r.at[2])
        for f in range(2):
            a, b = ((x, z), (z, x))[f]
            for d in (0, 1):
                to = (b + (1, 3)[d]) % 4
                part = pl.ds(4 * d, 4)
                for r in range(4):
                    gm_out[f, d, 4 * d + r] = referred(f, to, 4 * d + r) + gt_in[f, d, r]
                send(gm_out.at[f, d, part], gm_in.at[f, d, part], g_s.at[3], g_r.at[3], ahead(f, a, to))

    w = [Chunk(j) for j in range(CHUNKS)]

    for cp in in_pool:
        cp.wait()
    pool1()
    for cp in in_w[0]:
        cp.wait()
    w[0].s1()
    for cp in in_q:
        cp.wait()
    for i, src in enumerate((q_ref, do_ref)):
        send(src.at[pl.ds(0, SPAN)], halo.at[i], h_s.at[0], h_r.at[0], ((c + 15) % 16, e))
    pool2()
    for pair in in_w[1:]:
        for cp in pair:
            cp.wait()
    for cp in in_small:
        cp.wait()
    w[0].s2()
    w[1].s1()
    pool3()

    def table(p, _):
        first, last, count = jnp.int32(0), jnp.int32(0), jnp.int32(0)
        r_first, r_last, r_count = jnp.int32(0), jnp.int32(0), jnp.int32(0)
        for r in range(8):
            hit = owner_ref[r % 2, c * 4 + r // 2] == p
            first = jnp.where(hit & (count == 0), r, first)
            last = jnp.where(hit, r, last)
            count = count + hit.astype(jnp.int32)
            there = owner_ref[r % 2, p * 4 + r // 2] == c
            n = slot_ref[r % 2, p * 4 + r // 2]
            r_first = jnp.where(there & (r_count == 0), n, r_first)
            r_last = jnp.where(there, n, r_last)
            r_count = r_count + there.astype(jnp.int32)
        stab[0, p], stab[1, p], stab[2, p] = first, last, count
        stab[3, p] = jnp.where(r_count > 0, r_first, -1)
        stab[4, p] = jnp.where(r_count > 1, r_last, -1)
        return 0

    lax.fori_loop(0, 16, table, 0)

    landed(halo, h_r.at[0])
    keep = jnp.where(c == 15, 0.0, 1.0)
    first_row = lax.broadcasted_iota(jnp.int32, (4 * SPAN, DH), 0) == 0

    def windows(ref, which, cols):
        own_rows = ref[:, cols].astype(F32)
        nxt = halo[which, :, cols].astype(F32) * keep
        shifted = pltpu.roll(jnp.concatenate([own_rows[SPAN:], nxt], axis=0), 1, 0)
        return jnp.where(first_row, own_rows[SPAN - 1 : SPAN], shifted)

    qcos = jnp.concatenate([cos_ref[0:SPAN, :]] * 4, axis=0)
    qsin = jnp.concatenate([sin_ref[0:SPAN, :]] * 4, axis=0)
    zero = jnp.zeros((SPAN, DH), BF16)

    def prepare(h):
        j, hh = h // 2, h % 2
        cols = pl.ds(h * DH, DH)
        v = windows(q_ref, 0, cols)
        qwin[h] = v
        xhat, _ = unit(v)
        rot = (rope(xhat * qg_ref[:, cols], qcos, qsin) * SCALE).astype(BF16)
        dov = windows(do_ref, 1, cols).astype(BF16)
        for s in range(4):
            r = slice(s * SPAN, (s + 1) * SPAN)
            mine = slice(hh * DH, (hh + 1) * DH)
            rest = slice((1 - hh) * DH, (2 - hh) * DH)
            rows = slice(hh * SPAN, (hh + 1) * SPAN)
            qbd[j, s, rows, mine] = rot[r]
            qbd[j, s, rows, rest] = zero
            dobd[j, s, rows, mine] = dov[r]
            dobd[j, s, rows, rest] = zero

    for h in range(4):
        prepare(h)
    pool4()
    w[0].s3()
    for h in range(4, 8):
        prepare(h)


    def to_sibling(f, slot):
        ref = ebuf.at[f, slot]
        send(ref, ref, e_s.at[2], e_r.at[f, 2], other)

    def y1(f):
        b = (z, x)[f]
        for r in range(8):
            ebuf[f, e, r * NT : (r + 1) * NT, :] = referred(f, b, r) + gm_in[f, 0, r] + gm_in[f, 1, r]
        for to in (up, dn):
            ref = ebuf.at[f, e]
            send(ref, ref, e_s.at[0], e_r.at[f, 0], (c, enc(to, core)))
        to_sibling(f, e)

    def y2(f):
        landed(ebuf.at[f, pl.ds(0, 2)], e_r.at[f, 0])
        for d, frm, to in ((0, dn, up), (1, up, dn)):
            slot = enc(frm, core)
            part = ebuf.at[f, slot, pl.ds(512 * d, 512)]
            send(part, part, e_s.at[1], e_r.at[f, 1], (c, enc(to, core)))
            to_sibling(f, slot)

    def y3(f):
        landed(ebuf.at[f, 0], e_r.at[f, 1])
        to_sibling(f, enc(opp, core))

    landed(gm_in, g_r.at[3])
    y1(0)
    y1(1)
    w[1].s2()
    w[3].s1()
    w[2].s1()
    w[1].s3()
    w[2].s2()
    w[3].s2()
    y2(0)
    w[0].s4()
    y2(1)
    w[2].s3()
    y3(0)
    y3(1)
    w[1].s4()
    w[0].done()
    for f in range(2):
        landed(ebuf.at[f, pl.ds(0, 4)], e_r.at[f, 2])

    def line_part(s, zi, xi):
        rows = slice(s * 256, (s + 1) * 256)
        j = CHUNKS - 1
        e_key = jnp.concatenate([ebuf[i % 2, 2 * zi + i // 2, rows, :] for i in range(4)], axis=1)
        e_value = jnp.concatenate([ebuf[xi % 2, 2 * i + xi // 2, rows, :] for i in range(4)], axis=1)
        return (
            jnp.dot(e_key, kw_all[j, zi].reshape(512, CW), preferred_element_type=F32),
            jnp.dot(e_value, vw_all[j, :, xi].reshape(512, CW), preferred_element_type=F32),
        )

    def project_early():
        for s in range(4):
            parts = [line_part(s, (z + d) % 4, (x + d) % 4) for d in (0, 1, 3)]
            early[0, s] = parts[0][0] + parts[1][0] + parts[2][0]
            early[1, s] = parts[0][1] + parts[1][1] + parts[2][1]

    def project(j, s):
        if j == CHUNKS - 1:
            key, value = line_part(s, (z + 2) % 4, (x + 2) % 4)
            kps[s % 2] = (early[0, s] + key).astype(BF16).astype(F32)
            vps[s % 2] = (early[1, s] + value).astype(BF16)
            return
        rows = slice(s * 256, (s + 1) * 256)
        ecat = jnp.concatenate([ebuf[f, i, rows, :] for i in range(8) for f in range(2)], axis=1)
        kw, vw = kw_all[j].reshape(2048, CW), vw_all[j].reshape(2048, CW)
        kps[s % 2] = jnp.dot(ecat, kw, preferred_element_type=F32).astype(BF16).astype(F32)
        vps[s % 2] = jnp.dot(ecat, vw, preferred_element_type=F32).astype(BF16)

    def keep_rows(s, cols, v):
        for rr in range(2):
            for h in range(2):
                to = h * 512 + (2 * s + rr) * 64
                dkv[to : to + 64, cols] = v[rr * NT + h * 64 : rr * NT + h * 64 + 64]

    def attend(j, s):
        rows = slice(s * 256, (s + 1) * 256)
        kp, vp = kps[s % 2], vps[s % 2]
        cos, sin = cos_ref[...], sin_ref[...]
        hats, rs, gains, ks = [], [], [], []
        for hh in range(2):
            xhat, r = unit(kp[:, hh * DH : (hh + 1) * DH])
            g = kg_ref[:, (2 * j + hh) * DH : (2 * j + hh + 1) * DH]
            ks.append(rope(xhat * g, cos, sin).astype(BF16))
            hats.append(xhat)
            rs.append(r)
            gains.append(g)
        k = jnp.concatenate(ks, axis=1)
        qb, dob = qbd[j, s], dobd[j, s]
        scores = lax.dot_general(k, qb, NT_DIMS, preferred_element_type=F32)
        dp = lax.dot_general(vp, dob, NT_DIMS, preferred_element_type=F32)
        p = jnp.exp(scores)
        p = p * (1.0 / jnp.sum(p, axis=0, keepdims=True))
        ds = (p * (dp - jnp.sum(p * dp, axis=0, keepdims=True))).astype(BF16)
        dv = jnp.dot(p.astype(BF16), dob, preferred_element_type=F32)
        dk = jnp.dot(ds, qb, preferred_element_type=F32)
        dq = lax.dot_general(ds, k, TN_DIMS, preferred_element_type=F32) * SCALE
        for hh in range(2):
            cols = slice(hh * DH, (hh + 1) * DH)
            d = rope_back(dk[:, cols], cos, sin) * gains[hh]
            keep_rows(s, cols, unit_back(d, hats[hh], rs[hh]).astype(BF16))
        keep_rows(s, slice(CW, 2 * CW), dv.astype(BF16))
        qrows = slice(s * SPAN, (s + 1) * SPAN)
        for hh in range(2):
            h = 2 * j + hh
            xhat, r = unit(qwin[h, qrows, :])
            d = dq[hh * SPAN : (hh + 1) * SPAN, hh * DH : (hh + 1) * DH]
            d = rope_back(d, cos_ref[0:SPAN, :], sin_ref[0:SPAN, :]) * qg_ref[:, h * DH : (h + 1) * DH]
            dqwin[qrows, h * DH : (h + 1) * DH] = unit_back(d, xhat, r)

    def compute(j, part):
        if part == 0:
            project(j, 0)
        for s in (2 * part, 2 * part + 1):
            if s < 3:
                project(j, s + 1)
            attend(j, s)

    def product(j, f, which, start=0, size=1024):
        xi = 2 * (core if which else 1 - core) + f
        for i in range(2):
            wcat = jnp.concatenate([b[j, 2 * i : 2 * i + 2, xi].reshape(256, CW) for b in (kw_all, vw_all)], axis=1)
            rows = slice(start, start + size)
            part = lax.dot_general(dkv[rows, :], wcat, NT_DIMS, preferred_element_type=F32)
            for k in range(2):
                new = part[:, k * 128 : (k + 1) * 128]
                if j > 0:
                    new = new + acc[f, which, 2 * i + k, rows, :]
                if j == CHUNKS - 1 and which == 0:
                    sib_out[f, 2 * i + k, rows, :] = new.astype(BF16)
                else:
                    acc[f, which, 2 * i + k, rows, :] = new

    def products(j):
        for f in range(2):
            for which in range(2):
                product(j, f, which)

    def query_rows(j):
        for h in (2 * j, 2 * j + 1):
            cols = slice(h * DH, (h + 1) * DH)
            back = pltpu.roll(dqwin[:, cols], 4 * SPAN - 1, 0).astype(BF16)
            qgrad_ref[SPAN:, cols] = back[: 3 * SPAN]
            qback_out[:, cols] = back[3 * SPAN :]

    compute(0, 0)
    compute(0, 1)
    w[2].s4()
    products(0)
    w[3].s3()
    w[1].done()
    compute(1, 0)
    compute(1, 1)
    products(1)
    w[2].done()
    compute(2, 0)
    w[3].s4()
    compute(2, 1)
    products(2)
    project_early()
    w[3].done()
    compute(3, 0)
    compute(3, 1)

    def rs_send(p, k, src, dst, to):
        send(src, dst, rs_s.at[k], rs_r.at[p, k], to)

    def rs_a(p):
        f, h = p // 2, p % 2
        product(CHUNKS - 1, f, 0, 512 * h, 512)
        rows = pl.ds(512 * h, 512)
        rs_send(p, 0, sib_out.at[f, :, rows], sib_in.at[f, :, rows], other)
        product(CHUNKS - 1, f, 1, 512 * h, 512)

    def both(p, i, start, size):
        rows = pl.ds(512 * (p % 2) + start, size)
        return acc[p // 2, 1, i, rows, :] + sib_in[p // 2, i, rows, :].astype(F32)

    sides = ((0, up), (1, dn))

    def rs_b(p):
        landed(sib_in.at[p // 2, :, pl.ds(512 * (p % 2), 512)], rs_r.at[p, 0])
        for d, to in sides:
            t_out[p, d] = both(p, opp, 256 * d, 256).astype(BF16)
            rs_send(p, 1, t_out.at[p, d], t_in.at[p, d], (c, enc(to, core)))
        for d, to in sides:
            m_out[p, d, 1 - d] = both(p, to, 256 * (1 - d), 256).astype(BF16)
            rs_send(p, 2, m_out.at[p, d, 1 - d], m_in.at[p, d, 1 - d], (c, enc(to, core)))

    def rs_c(p):
        landed(t_in.at[p], rs_r.at[p, 1])
        for d, to in sides:
            m_out[p, d, d] = (both(p, to, 256 * d, 256) + t_in[p, d].astype(F32)).astype(BF16)
            rs_send(p, 2, m_out.at[p, d, d], m_in.at[p, d, d], (c, enc(to, core)))

    def rs_d(p):
        landed(m_in.at[p], rs_r.at[p, 2])
        for h in range(2):
            total = both(p, y, 256 * h, 256) + m_in[p, 0, h].astype(F32) + m_in[p, 1, h].astype(F32)
            refg[p, 4 * h : 4 * h + 4] = total.astype(BF16).reshape(4, 64, 128)
        for d in (0, 10, 9, 11, 6, 14, 5, 7, 13, 15, 8, 2, 1, 3, 4, 12):
            to = (z + d // 4) % 4 * 4 + (x + d % 4) % 4
            count = stab[2, to]
            none = jnp.zeros((64, 128), BF16)
            block0 = jnp.where(count > 0, refg[p, stab[0, to]], none)
            block1 = jnp.where(count > 1, refg[p, stab[1, to]], none)
            if d == 0:
                ret_in[p, c, 0] = block0
                ret_in[p, c, 1] = block1
                continue
            ret_out[p, d, 0] = block0
            ret_out[p, d, 1] = block1
            send(ret_out.at[p, d], ret_in.at[p, c], ret_s.at[0], ret_r.at[p], (to, e))

    def rs_e(p):
        landed(ret_in.at[p, pl.ds(0, 15)], ret_r.at[p])

        def add(o, sums):
            b0, b1 = ret_in[p, o, 0].astype(F32), ret_in[p, o, 1].astype(F32)
            n0, n1 = stab[3, o], stab[4, o]
            return tuple(
                a + b0 * jnp.where(n0 == n, 1.0, 0.0) + b1 * jnp.where(n1 == n, 1.0, 0.0)
                for n, a in enumerate(sums)
            )

        for n, a in enumerate(lax.fori_loop(0, 16, add, tuple(jnp.zeros((64, 128), F32) for _ in range(4)))):
            sgrad_ref[n, 64 * (p % 2) : 64 * (p % 2) + 64, 128 * (p // 2) : 128 * (p // 2) + 128] = a

    rs_a(0)
    rs_b(0)
    for j in range(CHUNKS):
        query_rows(j)
    send(qback_out, qback, h_s.at[1], h_r.at[1], ((c + 1) % 16, e))
    rs_a(1)
    rs_c(0)
    rs_b(1)
    rs_a(2)
    rs_d(0)
    rs_c(1)
    rs_b(2)
    rs_a(3)
    rs_d(1)
    rs_c(2)
    rs_b(3)
    rs_d(2)
    rs_c(3)
    rs_d(3)

    landed(qback, h_r.at[1])
    live = jnp.where(c == 0, 0.0, 1.0)
    last_row = lax.broadcasted_iota(jnp.int32, (SPAN, DH), 0) == SPAN - 1
    for h in range(8):
        cols = slice(h * DH, (h + 1) * DH)
        head = qback[:, cols].astype(F32) * live
        qgrad_ref[0:SPAN, cols] = jnp.where(last_row, dqwin[0:1, cols], head).astype(BF16)

    for p in range(4):
        rs_e(p)
    sent(halo, h_s.at[0])
    sent(qback, h_s.at[1])
    for step, ref in enumerate((line.at[0], line.at[0, pl.ds(0, 2)], gt_out, gm_out)):
        sent(ref, g_s.at[step])
    for step, ref in enumerate((kw_all.at[0], kw_all.at[0, pl.ds(0, 2)], kw_all, kw_all.at[pl.ds(0, 2)])):
        sent(ref, w_s.at[step])
    for step, ref in enumerate((ebuf.at[0, pl.ds(0, 4)], ebuf.at[0, pl.ds(0, 2)], ebuf.at[0])):
        sent(ref, e_s.at[step])
    for step, ref in enumerate((sib_out, t_out, m_out)):
        sent(ref, rs_s.at[step])
    sent(ret_out.at[:, pl.ds(0, 15)], ret_s.at[0])


def shards(queries, out_grad, nbr_states, key_weight, value_weight, q_gain, k_gain, nbr_owner, nbr_slot):
    cos, sin = rope_tables()
    hbm = pl.BlockSpec(memory_space=pl.ANY)
    dma = pltpu.SemaphoreType.DMA
    vmem = pltpu.VMEM
    whole = pl.BlockSpec(memory_space=pltpu.VMEM)
    return pl.pallas_call(
        kernel,
        out_shape=(
            vmem((256, 1024), BF16),
            vmem((4, NT, 256), F32),
        ),
        in_specs=[hbm] * 11,
        out_specs=(whole, whole),
        scratch_shapes=[
            vmem((256, 1024), BF16),
            vmem((256, 1024), BF16),
            vmem((1, 1024), F32),
            vmem((1, 1024), F32),
            vmem((256, DH), F32),
            vmem((256, DH), F32),
            vmem((2, 4, 4, NT, 128), BF16),
            vmem((2, 2, 4, NT, 128), BF16),
            vmem((2, 2, 4, NT, 128), BF16),
            vmem((2, 2, 8, NT, 128), BF16),
            vmem((2, 2, 8, NT, 128), BF16),
            vmem((CHUNKS, 4, 4, 128, CW), BF16),
            vmem((CHUNKS, 4, 4, 128, CW), BF16),
            vmem((2, 8, 1024, 128), BF16),
            vmem((2, SPAN, 1024), BF16),
            vmem((8, 4 * SPAN, DH), F32),
            vmem((4, 4, 2 * SPAN, 256), BF16),
            vmem((4, 4, 2 * SPAN, 256), BF16),
            vmem((4 * SPAN, 1024), F32),
            vmem((SPAN, 1024), BF16),
            vmem((SPAN, 1024), BF16),
            vmem((1024, 2 * CW), BF16),
            vmem((2, 256, CW), F32),
            vmem((2, 256, CW), BF16),
            vmem((2, 4, 256, CW), F32),
            vmem((2, 2, 4, 1024, 128), F32),
            vmem((2, 4, 1024, 128), BF16),
            vmem((2, 4, 1024, 128), BF16),
            vmem((4, 2, 256, 128), BF16),
            vmem((4, 2, 256, 128), BF16),
            vmem((4, 2, 2, 256, 128), BF16),
            vmem((4, 2, 2, 256, 128), BF16),
            vmem((4, 8, 64, 128), BF16),
            vmem((4, 16, 2, 64, 128), BF16),
            vmem((4, 16, 2, 64, 128), BF16),
            pltpu.SMEM((5, 16), jnp.int32),
            pltpu.SMEM((2, 64), jnp.int32),
            pltpu.SMEM((2, 64), jnp.int32),
            dma((18,)),
            dma((4,)),
            dma((CHUNKS, 4)),
            dma((4,)),
            dma((4,)),
            dma((3,)),
            dma((2, 3)),
            dma((2,)),
            dma((2,)),
            dma((3,)),
            dma((4, 3)),
            dma((1,)),
            dma((4,)),
        ],
        compiler_params=pltpu.CompilerParams(
            collective_id=0, has_side_effects=True, vmem_limit_bytes=56 * 2**20
        ),
    )(
        queries, out_grad, nbr_states, key_weight, value_weight,
        q_gain.reshape(1, -1), k_gain.reshape(1, -1), jnp.asarray(cos), jnp.asarray(sin),
        nbr_owner.T, nbr_slot.T,
    )


def solution(mesh):
    in_specs = (
        P("ctx", "enc"),
        P("ctx", "enc"),
        P("ctx", None, "enc"),
        P("ctx", "enc"),
        P("ctx", "enc"),
        P("enc"),
        P("enc"),
        P(),
        P(),
    )
    out_specs = (P("ctx", "enc"), P("ctx", None, "enc"))
    return jax.shard_map(shards, mesh=mesh, in_specs=in_specs, out_specs=out_specs, check_vma=False)
```
